32 devices in a mesh: group: 2 (over y), ctx: 8 (over z, core), head: 2 (over x).
Axes of the slice: x: 2, y: 2, z: 4, core: 2. Of those that a mesh axis runs over, the one named last changes fastest.
Arguments:
- queries: bfloat16 [2048, 4096], P(('group', 'ctx'), 'head'), parts along dimension 0, may hold values from -6 to 6
- keys: bfloat16 [2048, 512], P(('group', 'ctx'), 'head'), parts along dimension 0, may hold values from -6 to 6
- values: bfloat16 [2048, 512], P(('group', 'ctx'), 'head'), parts along dimension 0, may hold values from -6 to 6
- sinks: float32 [64], P('head'), may hold values from 0 to 4
- segments: int32 [2048], P('group'), parts along dimension 0, may hold values from 0 to 3, never falling along the last dimension, each value on 1 to 768 neighbouring positions
- hidden_in: bfloat16 [2048, 2880], P(('group', 'ctx')), parts along dimension 0, may hold values from -6 to 6
- routes: int32 [2048, 4], P(('group', 'ctx')), parts along dimension 0, may hold values from 0 to 7, all different within a row; in each aligned block of 64 rows (0 to 63, 64 to 127, ...) at most 48 rows name the same one
- w_out: bfloat16 [4096, 2880], P('head'), may hold values from -0.09375 to 0.09375
- norm_gain: float32 [2880], replicated, may hold values from 0.1 to 1.9
- router: bfloat16 [2880, 8], replicated, may hold values from -0.109375 to 0.109375
- w_gate_up: bfloat16 [8, 2, 2880, 2880], P('ctx', None, None, 'head'), may hold values from -0.109375 to 0.109375
- w_down: bfloat16 [8, 2880, 2880], P('ctx', 'head'), may hold values from -0.109375 to 0.109375
Outputs:
- layer_out: bfloat16 [2048, 2880], P(('group', 'ctx', 'head')), parts along dimension 0
The draws below stay inside these ranges and needn't reach their ends.
There are 2 independent parts, one for each index of `group`. The reference program is written for one: setup_inputs(seed, part) draws one part's arguments, and reference() takes and returns one part's arrays. A program takes and returns all parts, laid end to end along the dimension named above; an argument that names none is the same for every part. Nothing has to cross between parts.
Inputs may be any that keep to these rules, and one draw needn't show every extreme that they name: `routes`: each row names 4 different experts; in each aligned block of 64 rows no expert is named by more than 48 rows, a bound that some block reaches. `segments`: requests fill consecutive positions in order; the longest has 768 positions.
All inputs are finite; a program needn't handle non-finite values.
Results may differ from the reference program's by a relative error of at most 0.015.
Values may be sent and summed in bfloat16 or wider, within the bound.
No kernel may reach another device: no remote copies, remote signals or barrier semaphores. Data moves between devices by JAX's collectives and lax.ppermute only.
A program may use at most 128 MiB of HBM per device.

```python
import math
import jax
import jax.numpy as jnp
import numpy as np
from jax import lax

D = 2880
QUERY_HEADS = 64
KEY_VALUE_HEADS = 8
HEAD_SIZE = 64
FF = 2880
TOPK = 4
TOTAL_POSITIONS = 1024
EXPERTS = 8
ROWS_DEV = 64
CAP = 48
SLICE = 1440
N_CTX = 8
N_HEAD = 2


def query_key_pair(key):
    first, second_choice = jax.random.split(key, 2)
    queries = jnp.clip(jax.random.normal(first, (TOTAL_POSITIONS, QUERY_HEADS * HEAD_SIZE), jnp.float32), -6.0, 6.0)
    keys = jnp.clip(jax.random.normal(second_choice, (TOTAL_POSITIONS, KEY_VALUE_HEADS * HEAD_SIZE), jnp.float32), -6.0, 6.0)
    return (queries, keys)


def draw_queries(key, part):
    return query_key_pair(key)[0].astype(jnp.bfloat16)


def draw_keys(key, part):
    return query_key_pair(key)[1].astype(jnp.bfloat16)


def shard_levels(own_key, shape, cuts, smallest, top_value):
    def one(dim, blocks):
        steps = jax.random.uniform(jax.random.fold_in(jax.random.fold_in(own_key, 6), dim), (blocks,), jnp.float32, smallest / len(cuts), top_value / len(cuts))
        return jnp.repeat(jnp.exp(steps), shape[dim] // blocks).reshape((-1,) + (1,) * (len(shape) - dim - 1))

    loudness = one(*cuts[0])
    for cut in cuts[1:]:
        loudness = loudness * one(*cut)
    return loudness


def split_up(count, total, reach, skew):
    portions = [(1 << 20) // math.isqrt(rank ** skew) + 1 for rank in range(2, count + 1)]
    surplus, holding = total - reach - (count - 1), [1] * (count - 1)
    while surplus > 0:
        free = [i for i in range(count - 1) if holding[i] < reach]
        whole, left = sum([portions[i] for i in free]), surplus
        for i in free:
            addition = min(reach - holding[i], max(1, left * portions[i] // whole), surplus)
            holding[i] = holding[i] + addition
            surplus = surplus - addition
    return np.array([reach] + holding)


def uneven_parts(stream_key, count, total, bound, skew):
    if count == 2:
        one = jax.random.randint(stream_key, (), max(1, total - bound), min(bound, total - 1) + 1)
        return jnp.stack([one, total - one])
    tallies = jnp.asarray(split_up(count, total, bound, skew), jnp.int32)
    twos = (count - 1) // 2
    donor, taker = tallies[1:1 + 2 * twos:2], tallies[2:2 + 2 * twos:2]
    margin = jnp.minimum(donor - 1, bound - taker)
    passed = jax.random.randint(jax.random.fold_in(stream_key, 1), (twos,), 0, 1 << 20) % (margin + 1)
    tallies = tallies.at[1:1 + 2 * twos:2].set(donor - passed).at[2:2 + 2 * twos:2].set(taker + passed)
    return tallies[jax.random.permutation(jax.random.fold_in(stream_key, 2), count)]


def deal_out(stream_key, own, number, rows, amount, top, limit, lean):
    ranking = jax.random.permutation(stream_key, amount)
    heavy_load, usual = load_shares(amount, rows * top, limit, lean, True), load_shares(amount, rows * top, limit, lean, False)
    places = jnp.arange(amount)

    def named(tallies, offset_by):
        used = int((tallies > 0).sum())
        fixed = max(1, used // 4)
        shifted = fixed + (places - fixed + offset_by * (used - fixed)) % max(1, amount - fixed)
        return jnp.zeros((amount,), jnp.int32).at[ranking[jnp.where(places < fixed, places, shifted)]].set(jnp.asarray(tallies, jnp.int32))

    tallies = jnp.where(number % 4 == 0, named(heavy_load, number // 4), named(usual, number - number // 4 - 1))
    mixed = jax.random.permutation(jax.random.fold_in(own, 3), amount)
    source_of, receiver = mixed[0:amount // 2 * 2:2], mixed[1:amount // 2 * 2:2]
    slack = jnp.minimum(tallies[source_of] - 1, limit - tallies[receiver]) // 2
    slack = jnp.where((source_of == ranking[0]) | (receiver == ranking[0]) | (tallies[receiver] == 0), 0, jnp.maximum(slack, 0))
    shifted = jax.random.randint(jax.random.fold_in(own, 4), (amount // 2,), 0, 1 << 20) % (slack + 1)
    tallies = tallies.at[source_of].add(-shifted).at[receiver].add(shifted)
    labels = jnp.searchsorted(jnp.cumsum(tallies), jnp.arange(rows * top), side="right").astype(jnp.int32)
    table = labels.reshape(top, rows).T
    table = table[jax.random.permutation(jax.random.fold_in(own, 1), rows)]
    offset_by = jax.random.randint(jax.random.fold_in(own, 2), (rows, 1), 0, top)
    return jnp.take_along_axis(table, (jnp.arange(top)[None, :] + offset_by) % top, axis=1)


def load_shares(amount, total, most, skew, full):
    portions = [(1 << 20) // math.isqrt(grade ** skew) + 1 for grade in range(1, amount + 1)]
    largest = most if full else min(most, max(-(-total // amount), total * portions[0] // sum(portions)))
    least = 1 if total - largest >= amount - 1 else 0
    counts, rest = [largest] + [least] * (amount - 1), total - largest - least * (amount - 1)
    while rest > 0:
        candidates = [i for i in range(1, amount) if counts[i] < largest] or [i for i in range(1, amount) if counts[i] < most]
        whole, remaining = sum([portions[i] for i in candidates]), rest
        for i in candidates:
            addition = min(most - counts[i], max(1, remaining * portions[i] // whole), rest)
            counts[i] = counts[i] + addition
            rest = rest - addition
    return np.array(counts)


def bell_draw(rng, extent, width, most, cuts=(), kind=jnp.bfloat16):
    values = jax.random.normal(rng, extent, jnp.float32) * width
    if len(cuts) > 0:
        values = shard_levels(rng, extent, cuts, -0.22, 0.18) * values
    return jnp.clip(values, min=-most, max=most).astype(kind)


def setup_inputs(seed: int = 0, part: int = 0) -> dict:
    key_of = jax.random.split(jax.random.key(seed), 13)
    part_keys = jax.random.split(jax.random.fold_in(key_of[12], part), 13)
    queries = draw_queries(jax.random.fold_in(jax.random.fold_in(key_of[12], part), 71), part)
    keys = draw_keys(jax.random.fold_in(jax.random.fold_in(key_of[12], part), 71), part)
    values = bell_draw(part_keys[2], (TOTAL_POSITIONS, KEY_VALUE_HEADS * HEAD_SIZE), 1.0, 6.0, ((0, 8), (1, 2)))
    sinks = jnp.clip(4.0 * jax.random.uniform(key_of[3], (QUERY_HEADS,), jnp.float32) ** shard_levels(key_of[3], (QUERY_HEADS,), ((0, 2),), -0.2, 0.2), 0.0, 4.0)
    segments = jnp.searchsorted(jnp.cumsum(uneven_parts(part_keys[4], 4, TOTAL_POSITIONS, 3 * TOTAL_POSITIONS // 4, 0)), jnp.arange(TOTAL_POSITIONS), side="right").astype(jnp.int32)
    hidden_in = bell_draw(part_keys[5], (TOTAL_POSITIONS, D), 1.0, 6.0, ((0, 8),))
    routes_keys = jax.random.split(jax.random.fold_in(part_keys[6], 1), TOTAL_POSITIONS // ROWS_DEV)
    routes_turns = jax.random.permutation(jax.random.fold_in(part_keys[6], 3), TOTAL_POSITIONS // ROWS_DEV)
    routes = jax.vmap(lambda own, number: deal_out(jax.random.fold_in(part_keys[6], 2), own, number, ROWS_DEV, EXPERTS, TOPK, CAP, 2))(routes_keys, routes_turns).reshape((TOTAL_POSITIONS, TOPK))
    w_out = bell_draw(key_of[7], (QUERY_HEADS * HEAD_SIZE, D), (QUERY_HEADS * HEAD_SIZE) ** -0.5, 0.09375, ((0, 2),))
    norm_gain = jnp.clip(1.0 + 0.18 * jax.random.normal(key_of[8], (D,), jnp.float32), 0.1, 1.9)
    router = bell_draw(key_of[9], (D, EXPERTS), D ** -0.5, 0.109375)
    w_gate_up = bell_draw(key_of[10], (EXPERTS, 2, D, FF), D ** -0.5, 0.109375, ((0, 8), (3, 2)))
    w_down = bell_draw(key_of[11], (EXPERTS, FF, D), FF ** -0.5, 0.109375, ((0, 8), (1, 2)))
    return {"queries": queries, "keys": keys, "values": values, "sinks": sinks, "segments": segments, "hidden_in": hidden_in, "routes": routes, "w_out": w_out, "norm_gain": norm_gain, "router": router, "w_gate_up": w_gate_up, "w_down": w_down}


masked_value = -1e+30

def reference(queries, keys, values, sinks, segments, hidden_in, routes, w_out, norm_gain, router, w_gate_up, w_down):
    group_share = QUERY_HEADS // KEY_VALUE_HEADS
    positions = jnp.arange(TOTAL_POSITIONS, dtype=jnp.int32)
    visible = (positions[None, :] <= positions[:, None]) & (segments[None, :] == segments[:, None])

    def key_value_share(kv_index):
        query_part = lax.dynamic_slice_in_dim(queries, kv_index * group_share * HEAD_SIZE, group_share * HEAD_SIZE, 1)
        query_part = query_part.reshape(TOTAL_POSITIONS, group_share, HEAD_SIZE).astype(jnp.float32)
        key_part = lax.dynamic_slice_in_dim(keys, kv_index * HEAD_SIZE, HEAD_SIZE, 1).astype(jnp.float32)
        value_part = lax.dynamic_slice_in_dim(values, kv_index * HEAD_SIZE, HEAD_SIZE, 1).astype(jnp.float32)
        sink_part = lax.dynamic_slice_in_dim(sinks, kv_index * group_share, group_share, 0)
        scores = jnp.einsum('tgd,nd->gtn', query_part, key_part) * HEAD_SIZE ** (-0.5)
        scores = jnp.where(visible[None], scores, masked_value)
        top_score = jnp.maximum(sink_part[:, None], lax.optimization_barrier(jnp.max(scores, axis=-1)))
        probs = jnp.where(visible[None], jnp.exp(scores - top_score[..., None]), 0.0)
        denom = lax.optimization_barrier(jnp.sum(probs, axis=-1)) + jnp.exp(sink_part[:, None] - top_score)
        probs_b = lax.optimization_barrier(probs.astype(jnp.bfloat16)).astype(jnp.float32)
        attended = jnp.einsum('gtn,nd->gtd', probs_b, value_part) / denom[..., None]
        return attended.astype(jnp.bfloat16).transpose(1, 0, 2)
    head_share = lax.map(key_value_share, jnp.arange(KEY_VALUE_HEADS, dtype=jnp.int32))
    attended = head_share.transpose(1, 0, 2, 3).reshape(TOTAL_POSITIONS, QUERY_HEADS * HEAD_SIZE)
    projected = jnp.dot(attended, w_out, preferred_element_type=jnp.float32)
    residual = (hidden_in.astype(jnp.float32) + projected).astype(jnp.bfloat16)
    widened = residual.astype(jnp.float32)
    normed = (widened * lax.rsqrt(lax.optimization_barrier(jnp.mean(widened * widened, axis=-1, keepdims=True)) + 1e-05) * norm_gain).astype(jnp.bfloat16)
    logits = jnp.dot(normed, router, preferred_element_type=jnp.float32)
    gates = jax.nn.softmax(jnp.take_along_axis(logits, routes, axis=1), axis=-1)
    rows_max = min(TOTAL_POSITIONS, N_CTX * N_HEAD * CAP)
    token_index = jnp.arange(TOTAL_POSITIONS, dtype=jnp.int32)

    def per_expert(carried, expert):
        chosen = routes == expert
        selected = jnp.any(chosen, axis=1)
        weight = lax.optimization_barrier(jnp.sum(jnp.where(chosen, gates, 0.0), axis=1))
        order_key = jnp.where(selected, token_index, TOTAL_POSITIONS + token_index)
        taken = jnp.argsort(order_key)[:rows_max].astype(jnp.int32)
        token_rows = normed[taken]
        gate_up = lax.dynamic_index_in_dim(w_gate_up, expert, 0, keepdims=False)
        down_full = lax.dynamic_index_in_dim(w_down, expert, 0, keepdims=False)
        gate_pre = jnp.dot(token_rows, gate_up[0], preferred_element_type=jnp.float32)
        up_pre = jnp.dot(token_rows, gate_up[1], preferred_element_type=jnp.float32)
        activation = (gate_pre * jax.nn.sigmoid(1.702 * gate_pre) * (up_pre + 1.0)).astype(jnp.bfloat16)
        act_slices = activation.reshape(rows_max, N_HEAD, SLICE).astype(jnp.float32)
        down_slices = down_full.reshape(N_HEAD, SLICE, D).astype(jnp.float32)
        pieces = jnp.einsum('msf,sfd->smd', act_slices, down_slices).astype(jnp.bfloat16)
        pieces = lax.optimization_barrier(pieces)
        expert_out = lax.optimization_barrier(jnp.sum(pieces.astype(jnp.float32), axis=0)).astype(jnp.bfloat16)
        contrib = weight[taken][:, None] * expert_out.astype(jnp.float32)
        return (carried.at[taken].add(contrib), None)
    mixture, _ = lax.scan(per_expert, jnp.zeros((TOTAL_POSITIONS, D), jnp.float32), jnp.arange(EXPERTS, dtype=jnp.int32))
    return (residual.astype(jnp.float32) + mixture).astype(jnp.bfloat16)
```

```python
import functools

import jax
import jax.numpy as jnp
from jax import lax
from jax.experimental import pallas as pl
from jax.experimental.pallas import tpu as pltpu
from jax.sharding import PartitionSpec as P

HEAD_SIZE = 64
LANES = 128
CORES = 2
MIB = 1 << 20

masked_value = -1e30
NT = (((1,), (1,)), ((), ()))
NN = (((1,), (0,)), ((), ()))


def dot(a, b, dims):
    return lax.dot_general(a, b, dims, preferred_element_type=jnp.float32)


def attend_kernel(
    n_ctx, own_rows, place, q_ref, kv_own, kv_sib, sink_ref, tok_seg, segments, w_ref, *rest
):
    n_head = len(rest) - 6
    outs = rest[:n_head]
    weights, bias, attended, ordered, sums, arrived = rest[n_head:]
    tok_count = q_ref.shape[0]
    features = w_ref.shape[0]
    step = weights.shape[1]
    copies = []
    for i in range(0, features, step):
        rows = min(step, features - i)
        copies.append(
            pltpu.make_async_copy(
                w_ref.at[pl.ds(i, rows)],
                weights.at[i // step, pl.ds(0, rows)],
                arrived.at[i // step],
            )
        )
        copies[-1].start()
    ctx, head = place[0], place[1]
    half = kv_own.shape[0]
    kv_width = kv_own.shape[1] // 2
    kv_groups = kv_width // HEAD_SIZE
    share = q_ref.shape[1] // kv_width
    first = jnp.sum((segments[...] < tok_seg[...]).astype(jnp.float32), axis=1, keepdims=True)
    tok = ctx * tok_count + lax.broadcasted_iota(jnp.int32, (tok_count, half), 0)
    lane = lax.broadcasted_iota(jnp.int32, (tok_count, half), 1)
    hop = lane // tok_count
    z_here = ctx // CORES
    z_from = z_here - hop
    z_from = jnp.where(z_from < 0, z_from + n_ctx // CORES, z_from)
    core = ctx - z_here * CORES
    for i in range(2):
        owner = z_from * CORES + (core if i == 0 else 1 - core)
        pos = owner * tok_count + (lane - hop * tok_count)
        seen = (pos <= tok) & (pos.astype(jnp.float32) >= first)
        bias[i] = jnp.where(seen, 0.0, masked_value)
    for g in range(kv_groups):
        span = slice(g * HEAD_SIZE, (g + 1) * HEAD_SIZE)
        vspan = slice(kv_width + g * HEAD_SIZE, kv_width + (g + 1) * HEAD_SIZE)
        k0, k1 = kv_own[:, span], kv_sib[:, span]
        v0, v1 = kv_own[:, vspan], kv_sib[:, vspan]
        for j in range(share):
            h = g * share + j
            hs = slice(h * HEAD_SIZE, (h + 1) * HEAD_SIZE)
            q = q_ref[:, hs] * jnp.asarray(HEAD_SIZE**-0.5, q_ref.dtype)
            s0 = dot(q, k0, NT) + bias[0]
            s1 = dot(q, k1, NT) + bias[1]
            sink = sink_ref[h]
            top = jnp.maximum(
                jnp.maximum(
                    jnp.max(s0, axis=1, keepdims=True), jnp.max(s1, axis=1, keepdims=True)
                ),
                sink,
            )
            p0 = jnp.exp(s0 - top)
            p1 = jnp.exp(s1 - top)
            denom = (
                jnp.sum(p0, axis=1, keepdims=True)
                + jnp.sum(p1, axis=1, keepdims=True)
                + jnp.exp(sink - top)
            )
            o = dot(p0.astype(jnp.bfloat16), v0, NN) + dot(p1.astype(jnp.bfloat16), v1, NN)
            attended[:, hs] = (o / denom).astype(jnp.bfloat16)
    for j in range(n_head):
        source = lax.rem(head + n_head - j, n_head) * own_rows
        ordered[j * own_rows : (j + 1) * own_rows, :] = attended[
            pl.ds(pl.multiple_of(source, own_rows), own_rows), :
        ]
    for i in range(0, features, step):
        rows = min(step, features - i)
        copies[i // step].wait()
        sums[:, i : i + rows] = dot(ordered[...], weights[i // step, :rows, :], NT).astype(
            jnp.bfloat16
        )
    for j in range(n_head):
        outs[j][...] = sums[j * own_rows : (j + 1) * own_rows, :]


def attend(place, q, kv_own, kv_sib, sinks, tok_seg, segments, w_out_t, n_ctx, n_head):
    tok_count, columns = q.shape
    features = w_out_t.shape[0]
    own_rows = tok_count // n_head
    step = min(features, 5 * LANES)
    parts = -(-features // step)
    vmem = pl.BlockSpec(memory_space=pltpu.VMEM)
    smem = pl.BlockSpec(memory_space=pltpu.SMEM)
    n_keys = 2 * kv_own.shape[0]
    return pl.pallas_call(
        functools.partial(attend_kernel, n_ctx, own_rows),
        out_shape=[jax.ShapeDtypeStruct((own_rows, features), jnp.bfloat16)] * n_head,
        in_specs=[smem, vmem, vmem, vmem, smem, vmem, vmem, pl.BlockSpec(memory_space=pl.ANY)],
        out_specs=[vmem] * n_head,
        scratch_shapes=[
            pltpu.VMEM((parts, step, columns), jnp.bfloat16),
            pltpu.VMEM((2, tok_count, kv_own.shape[0]), jnp.float32),
            pltpu.VMEM((tok_count, columns), jnp.bfloat16),
            pltpu.VMEM((tok_count, columns), jnp.bfloat16),
            pltpu.VMEM((tok_count, features), jnp.bfloat16),
            pltpu.SemaphoreType.DMA((parts,)),
        ],
        compiler_params=pltpu.CompilerParams(vmem_limit_bytes=40 * MIB),
        cost_estimate=pl.CostEstimate(
            flops=4 * tok_count * columns * n_keys + 2 * tok_count * columns * features,
            bytes_accessed=2 * columns * features,
            transcendentals=tok_count * n_keys * columns // HEAD_SIZE,
        ),
        name="attend",
    )(place, q, kv_own, kv_sib, sinks, tok_seg, segments, w_out_t)


def norm_kernel(experts, hidden, routes, gain, router, *refs):
    sums, (residual_out, rows_out) = refs[:-2], refs[-2:]
    features = hidden.shape[1]
    total = sums[0][...].astype(jnp.float32)
    for other in sums[1:]:
        total = total + other[...].astype(jnp.float32)
    residual = (hidden[...].astype(jnp.float32) + total).astype(jnp.bfloat16)
    residual_out[...] = residual
    widened = residual.astype(jnp.float32)
    scale_rows = lax.rsqrt(jnp.mean(widened * widened, axis=-1, keepdims=True) + 1e-05)
    normed = (widened * scale_rows * gain[...]).astype(jnp.bfloat16)
    logits = dot(normed, router[...], NT)
    tail = rows_out.shape[1] - LANES
    offset = features - tail
    lane = lax.broadcasted_iota(jnp.int32, logits.shape, 1)
    expert = lane - offset
    expert = jnp.where(expert >= experts, expert - experts, expert)
    named = routes[:, 0:1] == expert
    for k in range(1, routes.shape[1]):
        named = named | (routes[:, k : k + 1] == expert)
    high_lanes = (lane >= offset) & (lane < offset + experts)
    low_lanes = (lane >= offset + experts) & (lane < offset + 2 * experts)
    chosen = jnp.where(named & (high_lanes | low_lanes), logits, masked_value)
    top = jnp.max(chosen, axis=1, keepdims=True)
    weight = jnp.exp(chosen - top)
    denom = jnp.sum(jnp.where(high_lanes, weight, 0.0), axis=1, keepdims=True)
    gates = weight / denom
    high = gates.astype(jnp.bfloat16).astype(jnp.float32)
    packed = jnp.where(high_lanes, high, jnp.where(low_lanes, gates - high, 0.0))
    rows_out[:, :features] = normed
    end = rows_out[:, tail:].astype(jnp.float32)
    rows_out[:, tail:] = jnp.where(lane < offset, end, packed).astype(jnp.bfloat16)


def norm_and_gates(sums, hidden, routes, gain, router_lanes, experts, width):
    rows, features = hidden.shape
    vmem = pl.BlockSpec(memory_space=pltpu.VMEM)
    return pl.pallas_call(
        functools.partial(norm_kernel, experts),
        out_shape=[
            jax.ShapeDtypeStruct((rows, features), jnp.bfloat16),
            jax.ShapeDtypeStruct((rows, width), jnp.bfloat16),
        ],
        in_specs=[vmem] * (4 + len(sums)),
        out_specs=[vmem] * 2,
        cost_estimate=pl.CostEstimate(
            flops=rows * features * LANES * 2,
            bytes_accessed=rows * features * 10,
            transcendentals=rows * LANES,
        ),
        name="norm_and_gates",
    )(hidden, routes, gain, router_lanes, *sums)


def expert_kernel(experts, place, near, far, gate_up, down, near_out, far_out, rows, total):
    i = pl.program_id(0)
    features = down.shape[1]
    count = near.shape[0]

    @pl.when(i == 0)
    def _():
        rows[:count, :] = near[:, :features]
        rows[count:, :] = far[:, :features]

    gate_pre = dot(rows[...], gate_up[0], NT)
    up_pre = dot(rows[...], gate_up[1], NT)
    act = (gate_pre * jax.nn.sigmoid(1.702 * gate_pre) * (up_pre + 1.0)).astype(jnp.bfloat16)
    part = dot(act, down[...], NN)

    @pl.when(i == 0)
    def _():
        total[...] = part

    @pl.when(i > 0)
    def _():
        total[...] += part

    @pl.when(i == pl.num_programs(0) - 1)
    def _():
        tail = near.shape[1] - LANES
        lane = lax.broadcasted_iota(jnp.int32, (count, LANES), 1) - (features - tail)
        mine = (lane == place[0]) | (lane == place[0] + experts)
        for ref, out, start in ((near, near_out, 0), (far, far_out, count)):
            packed = ref[:, tail:].astype(jnp.float32)
            gate = jnp.sum(jnp.where(mine, packed, 0.0), axis=1, keepdims=True)
            out[...] = (total[start : start + count, :] * gate).astype(jnp.bfloat16)


def block_of(hidden_units):
    for size in range(256, 15, -16):
        if hidden_units % size == 0:
            return size
    return hidden_units


def expert_rows(place, near, far, gate_up_t, down, experts):
    count, width = near.shape
    hidden_units, features = down.shape
    block = block_of(hidden_units)
    whole = lambda i: (0, 0)
    return pl.pallas_call(
        functools.partial(expert_kernel, experts),
        grid=(hidden_units // block,),
        out_shape=[jax.ShapeDtypeStruct((count, features), jnp.bfloat16)] * 2,
        in_specs=[
            pl.BlockSpec(memory_space=pltpu.SMEM),
            pl.BlockSpec((count, width), whole),
            pl.BlockSpec((count, width), whole),
            pl.BlockSpec((2, block, features), lambda i: (0, i, 0)),
            pl.BlockSpec((block, features), lambda i: (i, 0)),
        ],
        out_specs=[pl.BlockSpec((count, features), whole)] * 2,
        scratch_shapes=[
            pltpu.VMEM((2 * count, features), jnp.bfloat16),
            pltpu.VMEM((2 * count, features), jnp.float32),
        ],
        compiler_params=pltpu.CompilerParams(vmem_limit_bytes=40 * MIB),
        cost_estimate=pl.CostEstimate(
            flops=12 * count * hidden_units * features,
            bytes_accessed=6 * hidden_units * features,
            transcendentals=2 * count * hidden_units,
        ),
        name="expert_rows",
    )(place, near, far, gate_up_t, down)


def body(
    queries,
    keys,
    values,
    sinks,
    segments,
    hidden_in,
    routes,
    w_out,
    norm_gain,
    router,
    w_gate_up,
    w_down,
):
    n_ctx = lax.axis_size("ctx")
    n_head = lax.axis_size("head")
    n_z = n_ctx // CORES
    ctx = lax.axis_index("ctx")
    head = lax.axis_index("head")
    tok_count = queries.shape[0]
    features = hidden_in.shape[1]
    experts = router.shape[1]
    own_rows = tok_count // n_head
    width = -(-(features + 2 * experts) // LANES) * LANES

    to_sibling = [(i, i ^ 1) for i in range(n_ctx)]
    to_next_chip = [(i, (i + CORES) % n_ctx) for i in range(n_ctx)]

    def sibling(x):
        return lax.ppermute(x, "ctx", to_sibling)

    def next_chip(x):
        return lax.ppermute(x, "ctx", to_next_chip)

    def next_head(x, j):
        return lax.ppermute(x, "head", [(i, (i + j) % n_head) for i in range(n_head)])

    def add(*terms):
        total = terms[0].astype(jnp.float32)
        for term in terms[1:]:
            total = total + term.astype(jnp.float32)
        return total.astype(jnp.bfloat16)

    place = jnp.stack([ctx, head]).astype(jnp.int32)
    row_start = head * own_rows
    own_hidden = lax.dynamic_slice_in_dim(hidden_in, row_start, own_rows, 0)
    own_routes = lax.dynamic_slice_in_dim(routes, row_start, own_rows, 0)
    tok_seg = lax.dynamic_slice_in_dim(segments, ctx * tok_count, tok_count, 0)[:, None]
    tail = features - (width - LANES)
    router_lanes = jnp.pad(
        jnp.concatenate([router.T, router.T]), ((tail, LANES - tail - 2 * experts), (0, 0))
    )
    gate_up_t = jnp.swapaxes(w_gate_up[0], 1, 2)
    down = w_down[0]

    with jax.named_scope("keys_and_values"):
        kv = [jnp.concatenate([keys, values], axis=1)]
        for _ in range(n_z - 1):
            kv.append(next_chip(kv[-1]))
        kv_own = jnp.concatenate(kv)
        kv_sib = sibling(kv_own)

    with jax.named_scope("attention"):
        sums = attend(
            place, queries, kv_own, kv_sib, sinks, tok_seg, segments[None, :], w_out.T, n_ctx, n_head
        )

    with jax.named_scope("norm"):
        gathered = [sums[0]] + [next_head(sums[j], n_head - j) for j in range(1, n_head)]
        residual, rows = norm_and_gates(
            gathered, own_hidden, own_routes, norm_gain[None, :], router_lanes, experts, width
        )

    with jax.named_scope("rows_of_chips"):
        from_chip = [rows]
        for _ in range(n_z - 1):
            from_chip.append(next_chip(from_chip[-1]))

    arriving = None
    for hop in list(range(1, n_z)) + [0]:
        with jax.named_scope("experts"):
            near = jnp.concatenate(
                [from_chip[hop]] + [next_head(from_chip[hop], j) for j in range(1, n_head)]
            )
            far = sibling(near)
            near_out, far_out = expert_rows(place, near, far, gate_up_t, down, experts)
        with jax.named_scope("sum_back"):
            crossed = sibling(far_out)
            blocks = [
                (
                    near_out[j * own_rows : (j + 1) * own_rows],
                    crossed[j * own_rows : (j + 1) * own_rows],
                )
                for j in range(n_head)
            ]
            terms = list(blocks[0])
            for j in range(1, n_head):
                terms.append(next_head(add(*blocks[j]), n_head - j))
            if arriving is not None:
                terms.append(arriving)
            if hop != 0:
                arriving = next_chip(add(*terms))
    return add(residual, *terms)


def solution(mesh):
    placed = (
        P(("group", "ctx"), "head"),
        P(("group", "ctx"), "head"),
        P(("group", "ctx"), "head"),
        P("head"),
        P("group"),
        P(("group", "ctx"), None),
        P(("group", "ctx"), None),
        P("head", None),
        P(),
        P(),
        P("ctx", None, None, "head"),
        P("ctx", "head", None),
    )
    return jax.shard_map(
        body,
        mesh=mesh,
        in_specs=placed,
        out_specs=P(("group", "ctx", "head"), None),
        check_vma=False,
    )
```

```python
import functools

import jax
import jax.numpy as jnp
from jax import lax
from jax.experimental import pallas as pl
from jax.experimental.pallas import tpu as pltpu
from jax.sharding import PartitionSpec as P

HEAD_SIZE = 64
LANES = 128
CORES = 2
VMEM_LIMIT = 16 << 20
UNITS = 4 * LANES
COLUMNS = 6 * LANES

masked_value = -1e30
NT = (((1,), (1,)), ((), ()))
NN = (((1,), (0,)), ((), ()))


def dot(a, b, dims):
    return lax.dot_general(a, b, dims, preferred_element_type=jnp.float32)


def load_kernel(n, *refs):
    sources, targets, flag, arrived = refs[:n], refs[-n - 2 : -2], refs[-2], refs[-1]
    flag[...] = jnp.zeros(flag.shape, flag.dtype)
    copies = [pltpu.make_async_copy(sources[i], targets[i], arrived.at[i]) for i in range(n)]
    for copy in copies:
        copy.start()
    for copy in copies:
        copy.wait()


def load(arrays, earlier):
    n = len(arrays)
    return pl.pallas_call(
        functools.partial(load_kernel, n),
        out_shape=[pltpu.VMEM(a.shape, a.dtype) for a in arrays]
        + [jax.ShapeDtypeStruct((8, LANES), jnp.float32)],
        in_specs=[pl.BlockSpec(memory_space=pl.ANY)] * n
        + [pl.BlockSpec(memory_space=pltpu.VMEM)],
        out_specs=[pl.BlockSpec(memory_space=pltpu.VMEM)] * (n + 1),
        scratch_shapes=[pltpu.SemaphoreType.DMA((n,))],
        compiler_params=pltpu.CompilerParams(vmem_limit_bytes=VMEM_LIMIT),
        cost_estimate=pl.CostEstimate(
            flops=0, bytes_accessed=sum(4 * a.size for a in arrays), transcendentals=0
        ),
        name="load",
    )(*[in_hbm(a) for a in arrays], earlier)


def in_hbm(x):
    return pltpu.with_memory_space_constraint(x, pltpu.HBM)


def in_vmem(x):
    return pltpu.with_memory_space_constraint(x, pltpu.VMEM)


def attend_kernel(n_ctx, n_head, place, q_ref, sink_ref, tok_seg, segments, w_ref, *rest):
    kv_refs, rest = rest[:n_ctx], rest[n_ctx:]
    outs, (kv, bias, attended, ordered, weights, arrived) = rest[:n_head], rest[n_head:]
    load_weights = pltpu.make_async_copy(w_ref, weights, arrived)
    load_weights.start()
    tok_count = q_ref.shape[0]
    own_rows = tok_count // n_head
    features = weights.shape[0]
    ctx, head = place[0], place[1]
    for i, ref in enumerate(kv_refs):
        kv[i * tok_count : (i + 1) * tok_count, :] = ref[...]
    keys = kv.shape[0]
    kv_width = kv.shape[1] // 2
    kv_groups = kv_width // HEAD_SIZE
    share = q_ref.shape[1] // kv_width
    first = jnp.sum((segments[...] < tok_seg[...]).astype(jnp.float32), axis=1, keepdims=True)
    tok = ctx * tok_count + lax.broadcasted_iota(jnp.int32, (tok_count, keys), 0)
    lane = lax.broadcasted_iota(jnp.int32, (tok_count, keys), 1)
    block = lane // tok_count
    hop = block // CORES
    z_here = ctx // CORES
    z_from = z_here - hop
    z_from = jnp.where(z_from < 0, z_from + n_ctx // CORES, z_from)
    core = ctx - z_here * CORES
    other = block - hop * CORES
    owner = z_from * CORES + jnp.where(other == 0, core, 1 - core)
    pos = owner * tok_count + (lane - block * tok_count)
    seen = (pos <= tok) & (pos.astype(jnp.float32) >= first)
    bias[...] = jnp.where(seen, 0.0, masked_value)
    for g in range(kv_groups):
        k = kv[:, g * HEAD_SIZE : (g + 1) * HEAD_SIZE]
        v = kv[:, kv_width + g * HEAD_SIZE : kv_width + (g + 1) * HEAD_SIZE]
        for j in range(share):
            h = g * share + j
            hs = slice(h * HEAD_SIZE, (h + 1) * HEAD_SIZE)
            q = q_ref[:, hs] * jnp.asarray(HEAD_SIZE**-0.5, q_ref.dtype)
            score = dot(q, k, NT) + bias[...]
            sink = sink_ref[h]
            top = jnp.maximum(jnp.max(score, axis=1, keepdims=True), sink)
            prob = jnp.exp(score - top)
            denom = jnp.sum(prob, axis=1, keepdims=True) + jnp.exp(sink - top)
            o = dot(prob.astype(jnp.bfloat16), v, NN)
            attended[:, hs] = (o / denom).astype(jnp.bfloat16)
    for j in range(n_head):
        source = lax.rem(head + n_head - j, n_head) * own_rows
        ordered[j * own_rows : (j + 1) * own_rows, :] = attended[
            pl.ds(pl.multiple_of(source, own_rows), own_rows), :
        ]
    width = outs[0].shape[1]
    for out in outs:
        out[:, width - LANES :] = jnp.zeros((own_rows, LANES), out.dtype)
    load_weights.wait()
    step = 5 * LANES
    for i in range(0, features, step):
        rows = min(step, features - i)
        part = dot(ordered[...], weights[i : i + rows, :], NT).astype(jnp.bfloat16)
        for j in range(n_head):
            outs[j][:, i : i + rows] = part[j * own_rows : (j + 1) * own_rows]


def attend(place, q, kv, sinks, tok_seg, segments, w_out_t, n_head, width):
    tok_count, columns = q.shape
    features = w_out_t.shape[0]
    own_rows = tok_count // n_head
    vmem = pl.BlockSpec(memory_space=pltpu.VMEM)
    smem = pl.BlockSpec(memory_space=pltpu.SMEM)
    n_ctx = len(kv)
    n_keys = n_ctx * tok_count
    return pl.pallas_call(
        functools.partial(attend_kernel, n_ctx, n_head),
        out_shape=[jax.ShapeDtypeStruct((own_rows, width), jnp.bfloat16)] * n_head,
        in_specs=[smem, vmem, smem, vmem, vmem, pl.BlockSpec(memory_space=pl.ANY)] + [vmem] * n_ctx,
        out_specs=[vmem] * n_head,
        scratch_shapes=[
            pltpu.VMEM((n_keys, kv[0].shape[1]), jnp.bfloat16),
            pltpu.VMEM((tok_count, n_keys), jnp.float32),
            pltpu.VMEM((tok_count, columns), jnp.bfloat16),
            pltpu.VMEM((tok_count, columns), jnp.bfloat16),
            pltpu.VMEM(w_out_t.shape, w_out_t.dtype),
            pltpu.SemaphoreType.DMA,
        ],
        compiler_params=pltpu.CompilerParams(vmem_limit_bytes=2 * VMEM_LIMIT),
        cost_estimate=pl.CostEstimate(
            flops=4 * tok_count * columns * n_keys + 2 * tok_count * columns * features,
            bytes_accessed=2 * columns * features,
            transcendentals=tok_count * n_keys * columns // HEAD_SIZE,
        ),
        name="attend",
    )(place, q, sinks, tok_seg, segments, in_hbm(w_out_t), *kv)


def norm_kernel(experts, hidden, routes, gain, router, *refs):
    sums, (residual_out, rows_out) = refs[:-2], refs[-2:]
    features = gain.shape[1]
    total = sums[0][...].astype(jnp.float32)
    for other in sums[1:]:
        total = total + other[...].astype(jnp.float32)
    residual = (hidden[...].astype(jnp.float32) + total).astype(jnp.bfloat16)
    residual_out[...] = residual
    widened = residual[:, :features].astype(jnp.float32)
    scale_rows = lax.rsqrt(jnp.mean(widened * widened, axis=-1, keepdims=True) + 1e-05)
    normed = (widened * scale_rows * gain[...]).astype(jnp.bfloat16)
    logits = dot(normed, router[...], NT)
    tail = rows_out.shape[1] - LANES
    offset = features - tail
    lane = lax.broadcasted_iota(jnp.int32, logits.shape, 1)
    expert = lane - offset
    expert = jnp.where(expert >= experts, expert - experts, expert)
    named = routes[:, 0:1] == expert
    for k in range(1, routes.shape[1]):
        named = named | (routes[:, k : k + 1] == expert)
    high_lanes = (lane >= offset) & (lane < offset + experts)
    low_lanes = (lane >= offset + experts) & (lane < offset + 2 * experts)
    chosen = jnp.where(named & (high_lanes | low_lanes), logits, masked_value)
    top = jnp.max(chosen, axis=1, keepdims=True)
    weight = jnp.exp(chosen - top)
    denom = jnp.sum(jnp.where(high_lanes, weight, 0.0), axis=1, keepdims=True)
    gates = weight / denom
    high = gates.astype(jnp.bfloat16).astype(jnp.float32)
    packed = jnp.where(high_lanes, high, jnp.where(low_lanes, gates - high, 0.0))
    rows_out[:, :features] = normed
    end = rows_out[:, tail:].astype(jnp.float32)
    rows_out[:, tail:] = jnp.where(lane < offset, end, packed).astype(jnp.bfloat16)


def norm_and_gates(sums, hidden, routes, gain, router_lanes, experts):
    rows, width = hidden.shape
    features = gain.shape[1]
    vmem = pl.BlockSpec(memory_space=pltpu.VMEM)
    return pl.pallas_call(
        functools.partial(norm_kernel, experts),
        out_shape=[jax.ShapeDtypeStruct((rows, width), jnp.bfloat16)] * 2,
        in_specs=[vmem] * (4 + len(sums)),
        out_specs=[vmem] * 2,
        compiler_params=pltpu.CompilerParams(vmem_limit_bytes=VMEM_LIMIT),
        cost_estimate=pl.CostEstimate(
            flops=rows * features * LANES * 2,
            bytes_accessed=rows * features * 10,
            transcendentals=rows * LANES,
        ),
        name="norm_and_gates",
    )(hidden, routes, gain, router_lanes, *sums)


def expert_kernel(experts, n_head, place, gate_up, down, flag, *refs):
    near, far = refs[:n_head], refs[n_head : 2 * n_head]
    outs, far_out, rows, hidden = refs[2 * n_head : -3], refs[-3], refs[-2], refs[-1]
    units, features = down.shape
    count, width = near[0].shape
    tail = width - LANES
    lane = lax.broadcasted_iota(jnp.int32, (count, LANES), 1) - (features - tail)
    mine = (lane == place[0]) | (lane == place[0] + experts)
    gates = []
    for i, ref in enumerate(near + far):
        rows[i * count : (i + 1) * count, :] = ref[:, :features]
        packed = ref[:, tail:].astype(jnp.float32)
        gates.append(jnp.sum(jnp.where(mine, packed, 0.0), axis=1, keepdims=True))
    for ref in (*outs, far_out):
        ref[:, tail:] = jnp.zeros((ref.shape[0], LANES), ref.dtype)
    for i in range(0, units, UNITS):
        end = min(units, i + UNITS)
        gate_pre = dot(rows[...], gate_up[0, i:end, :], NT)
        up_pre = dot(rows[...], gate_up[1, i:end, :], NT)
        act = gate_pre * jax.nn.sigmoid(1.702 * gate_pre) * (up_pre + 1.0)
        hidden[:, i:end] = act.astype(jnp.bfloat16)
    for i in range(0, features, COLUMNS):
        end = min(features, i + COLUMNS)
        part = dot(hidden[...], down[:, i:end], NN)
        for j in range(2 * n_head):
            block = (part[j * count : (j + 1) * count] * gates[j]).astype(jnp.bfloat16)
            if j < n_head:
                outs[j][:, i:end] = block
            else:
                far_out[(j - n_head) * count : (j - n_head + 1) * count, i:end] = block


def expert_rows(
                place, near, far, gate_up_t, down, flag, experts
            ):
    count, width = near[0].shape
    units, features = down.shape
    n_head = len(near)
    vmem = pl.BlockSpec(memory_space=pltpu.VMEM)
    return pl.pallas_call(
        functools.partial(expert_kernel, experts, n_head),
        out_shape=[jax.ShapeDtypeStruct((count, width), jnp.bfloat16)] * n_head
        + [jax.ShapeDtypeStruct((n_head * count, width), jnp.bfloat16)],
        in_specs=[pl.BlockSpec(memory_space=pltpu.SMEM)] + [vmem] * (3 + 2 * n_head),
        out_specs=[vmem] * (n_head + 1),
        scratch_shapes=[
            pltpu.VMEM((2 * n_head * count, features), jnp.bfloat16),
            pltpu.VMEM((2 * n_head * count, units), jnp.bfloat16),
        ],
        compiler_params=pltpu.CompilerParams(vmem_limit_bytes=VMEM_LIMIT),
        cost_estimate=pl.CostEstimate(
            flops=12 * n_head * count * units * features,
            bytes_accessed=6 * units * features,
            transcendentals=2 * n_head * count * units,
        ),
        name="expert_rows",
    )(place, in_vmem(gate_up_t), in_vmem(down), flag, *near, *far)


def body(
    queries,
    keys,
    values,
    sinks,
    segments,
    hidden_in,
    routes,
    w_out,
    norm_gain,
    router,
    w_gate_up,
    w_down,
):
    n_ctx = lax.axis_size("ctx")
    n_head = lax.axis_size("head")
    n_z = n_ctx // CORES
    ctx = lax.axis_index("ctx")
    head = lax.axis_index("head")
    tok_count = queries.shape[0]
    features = hidden_in.shape[1]
    experts = router.shape[1]
    own_rows = tok_count // n_head
    width = -(-(features + 2 * experts) // LANES) * LANES

    to_sibling = [(i, i ^ 1) for i in range(n_ctx)]
    to_next_chip = [(i, (i + CORES) % n_ctx) for i in range(n_ctx)]

    def sibling(x):
        return lax.ppermute(x, "ctx", to_sibling)

    def next_chip(x):
        return lax.ppermute(x, "ctx", to_next_chip)

    def next_head(x, j):
        return lax.ppermute(x, "head", [(i, (i + j) % n_head) for i in range(n_head)])

    def add(*terms):
        total = terms[0].astype(jnp.float32)
        for term in terms[1:]:
            total = total + term.astype(jnp.float32)
        return total.astype(jnp.bfloat16)

    def after(later, earlier):
        return lax.optimization_barrier((later, earlier))

    place = jnp.stack([ctx, head]).astype(jnp.int32)
    row_start = head * own_rows
    own_hidden = jnp.pad(
        lax.dynamic_slice_in_dim(hidden_in, row_start, own_rows, 0), ((0, 0), (0, width - features))
    )
    own_routes = lax.dynamic_slice_in_dim(routes, row_start, own_rows, 0)
    tok_seg = lax.dynamic_slice_in_dim(segments, ctx * tok_count, tok_count, 0)[:, None]
    tail = features - (width - LANES)
    router_lanes = jnp.pad(
        jnp.concatenate([router.T, router.T]), ((tail, LANES - tail - 2 * experts), (0, 0))
    )

    with jax.named_scope("keys_and_values"):
        own = jnp.concatenate([keys, values], axis=1)
        kv = [own, sibling(own)]
        for hop in range(1, n_z):
            own = next_chip(own)
            kv += [own, sibling(own)]

    with jax.named_scope("attention"):
        sums = attend(
            place, queries, kv, sinks, tok_seg, segments[None, :], w_out.T, n_head, width
        )

    with jax.named_scope("norm"):
        gathered = [sums[0]] + [next_head(sums[j], n_head - j) for j in range(1, n_head)]
        residual, rows = norm_and_gates(
            gathered, own_hidden, own_routes, norm_gain[None, :], router_lanes, experts
        )

    with jax.named_scope("rows_of_chips"):
        near = [rows] + [next_head(rows, j) for j in range(1, n_head)]
        from_chip = [rows, next_chip(rows)]
        down, gate_up_t, flag = load([w_down[0], jnp.swapaxes(w_gate_up[0], 1, 2)], rows)
        near, from_chip, flag = lax.optimization_barrier((near, from_chip, flag))
        for _ in range(n_z - 2):
            from_chip.append(next_chip(from_chip[-1]))

    lots = []
    before = None
    for hop in range(n_z):
        with jax.named_scope("experts"):
            if hop > 0:
                near = [from_chip[hop]]
                near += [next_head(from_chip[hop], j) for j in range(1, n_head)]
            far = [sibling(x) for x in near]
            if before is not None:
                near, before = after(near, before)
            *near_out, far_out = expert_rows(
                place, near, far, gate_up_t, down, flag, experts
            )
        with jax.named_scope("sum_back"):
            crossed = sibling(far_out)
            blocks = [
                (near_out[j], crossed[j * own_rows : (j + 1) * own_rows]) for j in range(n_head)
            ]
            if hop == 0:
                lots.append(blocks)
                before = far_out
            else:
                others = [add(*blocks[j]) for j in range(1, n_head)]
                lots.append([blocks[0]] + others)
                before = others
    own_blocks, before = after(lots[0][1:], before)
    lots[0] = [lots[0][0]] + [add(*block) for block in own_blocks]

    arriving = []
    for hop in list(range(1, n_z)) + [0]:
        with jax.named_scope("sum_back"):
            terms = list(lots[hop][0]) + arriving
            terms += [next_head(lots[hop][j], n_head - j) for j in range(1, n_head)]
            if hop != 0:
                arriving = [next_chip(add(*terms))]
    return add(residual, *terms)[:, :features]


def solution(mesh):
    placed = (
        P(("group", "ctx"), "head"),
        P(("group", "ctx"), "head"),
        P(("group", "ctx"), "head"),
        P("head"),
        P("group"),
        P(("group", "ctx"), None),
        P(("group", "ctx"), None),
        P("head", None),
        P(),
        P(),
        P("ctx", None, None, "head"),
        P("ctx", "head", None),
    )
    return jax.shard_map(
        body,
        mesh=mesh,
        in_specs=placed,
        out_specs=P(("group", "ctx", "head"), None),
        check_vma=False,
    )
```

```python
import functools

import jax
import jax.numpy as jnp
from jax import lax
from jax.experimental import pallas as pl
from jax.experimental.pallas import tpu as pltpu
from jax.sharding import PartitionSpec as P

HEAD_SIZE = 64
LANES = 128
CORES = 2
VMEM_LIMIT = 16 << 20
STACKED_HEADS = 4
UNITS = 4 * LANES
COLUMNS = 6 * LANES

masked_value = -1e30
NT = (((1,), (1,)), ((), ()))
NN = (((1,), (0,)), ((), ()))


def dot(a, b, dims):
    return lax.dot_general(a, b, dims, preferred_element_type=jnp.float32)


def load_kernel(n, *refs):
    sources, targets, flag, arrived = refs[:n], refs[-n - 2 : -2], refs[-2], refs[-1]
    flag[...] = jnp.zeros(flag.shape, flag.dtype)
    copies = [pltpu.make_async_copy(sources[i], targets[i], arrived.at[i]) for i in range(n)]
    for copy in copies:
        copy.start()
    for copy in copies:
        copy.wait()


def load(arrays, earlier):
    n = len(arrays)
    return pl.pallas_call(
        functools.partial(load_kernel, n),
        out_shape=[pltpu.VMEM(a.shape, a.dtype) for a in arrays]
        + [jax.ShapeDtypeStruct((8, LANES), jnp.float32)],
        in_specs=[pl.BlockSpec(memory_space=pl.ANY)] * n
        + [pl.BlockSpec(memory_space=pltpu.VMEM)],
        out_specs=[pl.BlockSpec(memory_space=pltpu.VMEM)] * (n + 1),
        scratch_shapes=[pltpu.SemaphoreType.DMA((n,))],
        compiler_params=pltpu.CompilerParams(vmem_limit_bytes=VMEM_LIMIT),
        cost_estimate=pl.CostEstimate(
            flops=0, bytes_accessed=sum(4 * a.size for a in arrays), transcendentals=0
        ),
        name="load",
    )(*[in_hbm(a) for a in arrays], earlier)


def in_hbm(x):
    return pltpu.with_memory_space_constraint(x, pltpu.HBM)


def in_vmem(x):
    return pltpu.with_memory_space_constraint(x, pltpu.VMEM)


def pack_kernel(left, right, both, arrived):
    half = left.shape[1]
    if half % LANES:
        both[:, :half] = left[...]
        both[:, half:] = right[...]
        return
    copies = [
        pltpu.make_async_copy(left, both.at[:, pl.ds(0, half)], arrived.at[0]),
        pltpu.make_async_copy(right, both.at[:, pl.ds(half, half)], arrived.at[1]),
    ]
    for copy in copies:
        copy.start()
    for copy in copies:
        copy.wait()


def side_by_side(left, right):
    rows, half = left.shape
    vmem = pl.BlockSpec(memory_space=pltpu.VMEM)
    source = vmem if half % LANES else pl.BlockSpec(memory_space=pl.ANY)
    return pl.pallas_call(
        pack_kernel,
        out_shape=jax.ShapeDtypeStruct((rows, 2 * half), left.dtype),
        in_specs=[source] * 2,
        out_specs=vmem,
        scratch_shapes=[pltpu.SemaphoreType.DMA((2,))],
        compiler_params=pltpu.CompilerParams(vmem_limit_bytes=VMEM_LIMIT),
        cost_estimate=pl.CostEstimate(
            flops=0, bytes_accessed=8 * rows * half, transcendentals=0
        ),
        name="side_by_side",
    )(*[x if half % LANES else in_hbm(x) for x in (left, right)])


def prepare_kernel(place, q_ref, tok_seg, segments, q_out, bias):
    tok_count = q_ref.shape[0]
    for h in range(q_ref.shape[1] // HEAD_SIZE):
        q_out[h * tok_count : (h + 1) * tok_count, :] = q_ref[
            :, h * HEAD_SIZE : (h + 1) * HEAD_SIZE
        ] * jnp.asarray(HEAD_SIZE**-0.5, q_ref.dtype)
    ctx = place[0]
    z_here = ctx // CORES
    core = ctx - z_here * CORES
    first = jnp.sum((segments[...] < tok_seg[...]).astype(jnp.float32), axis=1, keepdims=True)
    tok = ctx * tok_count + lax.broadcasted_iota(jnp.int32, bias.shape, 0)
    lane = lax.broadcasted_iota(jnp.int32, bias.shape, 1)
    block = lane // tok_count
    hop = block // CORES
    owner = (z_here - hop) * CORES + jnp.where(block == hop * CORES, core, 1 - core)
    pos = owner * tok_count + (lane - block * tok_count)
    seen = (z_here >= hop) & (pos <= tok) & (pos.astype(jnp.float32) >= first)
    bias[...] = jnp.where(seen, 0.0, masked_value)


def prepare(place, q, tok_seg, segments):
    tok_count, columns = q.shape
    vmem = pl.BlockSpec(memory_space=pltpu.VMEM)
    return pl.pallas_call(
        prepare_kernel,
        out_shape=[
            jax.ShapeDtypeStruct((columns // HEAD_SIZE * tok_count, HEAD_SIZE), q.dtype),
            jax.ShapeDtypeStruct((tok_count, segments.shape[1]), jnp.float32),
        ],
        in_specs=[pl.BlockSpec(memory_space=pltpu.SMEM)] + [vmem] * 3,
        out_specs=[vmem] * 2,
        compiler_params=pltpu.CompilerParams(vmem_limit_bytes=VMEM_LIMIT),
        cost_estimate=pl.CostEstimate(
            flops=20 * tok_count * segments.shape[1],
            bytes_accessed=4 * tok_count * segments.shape[1],
            transcendentals=0,
        ),
        name="prepare",
    )(place, q, tok_seg, segments)


def attend_kernel(n_ctx, n_head, place, sinks, q_ref, bias, w_ref, *rest):
    kv_refs, rest = rest[:n_ctx], rest[n_ctx:]
    outs, (probs, attended, ordered, weights, arrived) = rest[:n_head], rest[n_head:]
    load_weights = pltpu.make_async_copy(w_ref, weights, arrived)
    load_weights.start()
    tok_count = bias.shape[0]
    own_rows = tok_count // n_head
    features = weights.shape[0]
    kv_width = kv_refs[0].shape[1] // 2
    kv_groups = kv_width // HEAD_SIZE
    share = q_ref.shape[0] // tok_count // kv_groups
    stack = min(share, STACKED_HEADS)
    for g in range(kv_groups):
        ks = slice(g * HEAD_SIZE, (g + 1) * HEAD_SIZE)
        vs = slice(kv_width + g * HEAD_SIZE, kv_width + (g + 1) * HEAD_SIZE)
        k = jnp.concatenate([ref[:, ks] for ref in kv_refs])
        v = jnp.concatenate([ref[:, vs] for ref in kv_refs])
        for j in range(0, share, stack):
            heads = range(g * share + j, g * share + min(share, j + stack))
            scores = dot(q_ref[heads[0] * tok_count : (heads[-1] + 1) * tok_count, :], k, NT)
            denoms = []
            for i, h in enumerate(heads):
                score = scores[i * tok_count : (i + 1) * tok_count] + bias[...]
                top = jnp.maximum(jnp.max(score, axis=1, keepdims=True), sinks[h])
                prob = jnp.exp(score - top)
                denoms.append(jnp.sum(prob, axis=1, keepdims=True) + jnp.exp(sinks[h] - top))
                probs[(j + i) * tok_count : (j + i + 1) * tok_count, :] = prob.astype(jnp.bfloat16)
            out = dot(probs[j * tok_count : (j + len(heads)) * tok_count, :], v, NN)
            for i, h in enumerate(heads):
                attended[:, h * HEAD_SIZE : (h + 1) * HEAD_SIZE] = (
                    out[i * tok_count : (i + 1) * tok_count] / denoms[i]
                ).astype(jnp.bfloat16)
    head = place[1]
    for j in range(n_head):
        source = lax.rem(head + n_head - j, n_head) * own_rows
        ordered[j * own_rows : (j + 1) * own_rows, :] = attended[
            pl.ds(pl.multiple_of(source, own_rows), own_rows), :
        ]
    width = outs[0].shape[1]
    for out in outs:
        out[:, width - LANES :] = jnp.zeros((own_rows, LANES), out.dtype)
    load_weights.wait()
    for i in range(0, features, COLUMNS):
        end = min(features, i + COLUMNS)
        part = dot(ordered[...], weights[i:end, :], NT).astype(jnp.bfloat16)
        for j in range(n_head):
            outs[j][:, i:end] = part[j * own_rows : (j + 1) * own_rows]


def attend(place, sinks, q, bias, w_out_t, kv, n_head, width):
    tok_count, n_keys = bias.shape
    features, columns = w_out_t.shape
    own_rows = tok_count // n_head
    vmem = pl.BlockSpec(memory_space=pltpu.VMEM)
    smem = pl.BlockSpec(memory_space=pltpu.SMEM)
    share = columns // (kv[0].shape[1] // 2)
    return pl.pallas_call(
        functools.partial(attend_kernel, len(kv), n_head),
        out_shape=[jax.ShapeDtypeStruct((own_rows, width), jnp.bfloat16)] * n_head,
        in_specs=[smem, smem, vmem, vmem, pl.BlockSpec(memory_space=pl.ANY)] + [vmem] * len(kv),
        out_specs=[vmem] * n_head,
        scratch_shapes=[
            pltpu.VMEM((share * tok_count, n_keys), jnp.bfloat16),
            pltpu.VMEM((tok_count, columns), jnp.bfloat16),
            pltpu.VMEM((tok_count, columns), jnp.bfloat16),
            pltpu.VMEM(w_out_t.shape, w_out_t.dtype),
            pltpu.SemaphoreType.DMA,
        ],
        compiler_params=pltpu.CompilerParams(vmem_limit_bytes=2 * VMEM_LIMIT),
        cost_estimate=pl.CostEstimate(
            flops=4 * tok_count * columns * n_keys + 2 * tok_count * columns * features,
            bytes_accessed=2 * columns * features,
            transcendentals=tok_count * n_keys * columns // HEAD_SIZE,
        ),
        name="attend",
    )(place, sinks, q, bias, in_hbm(w_out_t), *kv)


def norm_kernel(experts, hidden, routes, gain, router, *refs):
    sums, (residual_out, rows_out) = refs[:-2], refs[-2:]
    features = gain.shape[1]
    total = sums[0][...].astype(jnp.float32)
    for other in sums[1:]:
        total = total + other[...].astype(jnp.float32)
    residual = (hidden[...].astype(jnp.float32) + total).astype(jnp.bfloat16)
    residual_out[...] = residual
    widened = residual[:, :features].astype(jnp.float32)
    scale_rows = lax.rsqrt(jnp.mean(widened * widened, axis=-1, keepdims=True) + 1e-05)
    normed = (widened * scale_rows * gain[...]).astype(jnp.bfloat16)
    logits = dot(normed, router[...], NT)
    tail = rows_out.shape[1] - LANES
    offset = features - tail
    lane = lax.broadcasted_iota(jnp.int32, logits.shape, 1)
    expert = lane - offset
    expert = jnp.where(expert >= experts, expert - experts, expert)
    named = routes[:, 0:1] == expert
    for k in range(1, routes.shape[1]):
        named = named | (routes[:, k : k + 1] == expert)
    high_lanes = (lane >= offset) & (lane < offset + experts)
    low_lanes = (lane >= offset + experts) & (lane < offset + 2 * experts)
    chosen = jnp.where(named & (high_lanes | low_lanes), logits, masked_value)
    top = jnp.max(chosen, axis=1, keepdims=True)
    weight = jnp.exp(chosen - top)
    denom = jnp.sum(jnp.where(high_lanes, weight, 0.0), axis=1, keepdims=True)
    gates = weight / denom
    high = gates.astype(jnp.bfloat16).astype(jnp.float32)
    packed = jnp.where(high_lanes, high, jnp.where(low_lanes, gates - high, 0.0))
    rows_out[:, :features] = normed
    end = rows_out[:, tail:].astype(jnp.float32)
    rows_out[:, tail:] = jnp.where(lane < offset, end, packed).astype(jnp.bfloat16)


def norm_and_gates(sums, hidden, routes, gain, router_lanes, experts):
    rows, width = hidden.shape
    features = gain.shape[1]
    vmem = pl.BlockSpec(memory_space=pltpu.VMEM)
    return pl.pallas_call(
        functools.partial(norm_kernel, experts),
        out_shape=[jax.ShapeDtypeStruct((rows, width), jnp.bfloat16)] * 2,
        in_specs=[vmem] * (4 + len(sums)),
        out_specs=[vmem] * 2,
        compiler_params=pltpu.CompilerParams(vmem_limit_bytes=VMEM_LIMIT),
        cost_estimate=pl.CostEstimate(
            flops=rows * features * LANES * 2,
            bytes_accessed=rows * features * 10,
            transcendentals=rows * LANES,
        ),
        name="norm_and_gates",
    )(hidden, routes, gain, router_lanes, *sums)


def expert_kernel(experts, n_head, place, gate_up, down, flag, *refs):
    near, far = refs[:n_head], refs[n_head : 2 * n_head]
    outs, (far_out, done, rows, hidden) = refs[2 * n_head : -4], refs[-4:]
    done[...] = flag[...]
    units, features = down.shape
    count, width = near[0].shape
    tail = width - LANES
    lane = lax.broadcasted_iota(jnp.int32, (count, LANES), 1) - (features - tail)
    mine = (lane == place[0]) | (lane == place[0] + experts)
    gates = []
    for i, ref in enumerate(near + far):
        rows[i * count : (i + 1) * count, :] = ref[:, :features]
        packed = ref[:, tail:].astype(jnp.float32)
        gates.append(jnp.sum(jnp.where(mine, packed, 0.0), axis=1, keepdims=True))
    for ref in (*outs, far_out):
        ref[:, tail:] = jnp.zeros((ref.shape[0], LANES), ref.dtype)
    for i in range(0, units, UNITS):
        end = min(units, i + UNITS)
        gate_pre = dot(rows[...], gate_up[0, i:end, :], NT)
        up_pre = dot(rows[...], gate_up[1, i:end, :], NT)
        act = gate_pre * jax.nn.sigmoid(1.702 * gate_pre) * (up_pre + 1.0)
        hidden[:, i:end] = act.astype(jnp.bfloat16)
    for i in range(0, features, COLUMNS):
        end = min(features, i + COLUMNS)
        part = dot(hidden[...], down[:, i:end], NN)
        for j in range(2 * n_head):
            block = (part[j * count : (j + 1) * count] * gates[j]).astype(jnp.bfloat16)
            if j < n_head:
                outs[j][:, i:end] = block
            else:
                far_out[(j - n_head) * count : (j - n_head + 1) * count, i:end] = block


def expert_rows(
                place, near, far, gate_up_t, down, flag, experts
            ):
    count, width = near[0].shape
    units, features = down.shape
    n_head = len(near)
    vmem = pl.BlockSpec(memory_space=pltpu.VMEM)
    return pl.pallas_call(
        functools.partial(expert_kernel, experts, n_head),
        out_shape=[jax.ShapeDtypeStruct((count, width), jnp.bfloat16)] * n_head
        + [jax.ShapeDtypeStruct((n_head * count, width), jnp.bfloat16)]
        + [jax.ShapeDtypeStruct(flag.shape, flag.dtype)],
        in_specs=[pl.BlockSpec(memory_space=pltpu.SMEM)] + [vmem] * (3 + 2 * n_head),
        out_specs=[vmem] * (n_head + 2),
        scratch_shapes=[
            pltpu.VMEM((2 * n_head * count, features), jnp.bfloat16),
            pltpu.VMEM((2 * n_head * count, units), jnp.bfloat16),
        ],
        compiler_params=pltpu.CompilerParams(vmem_limit_bytes=VMEM_LIMIT),
        cost_estimate=pl.CostEstimate(
            flops=12 * n_head * count * units * features,
            bytes_accessed=6 * units * features,
            transcendentals=2 * n_head * count * units,
        ),
        name="expert_rows",
    )(place, in_vmem(gate_up_t), in_vmem(down), flag, *near, *far)


def finish_kernel(flag, *refs):
    terms, out = refs[:-1], refs[-1]
    features = out.shape[1]
    total = terms[0][:, :features].astype(jnp.float32)
    for term in terms[1:]:
        total = total + term[:, :features].astype(jnp.float32)
    out[...] = total.astype(out.dtype)


def finish(flag, terms, features):
    vmem = pl.BlockSpec(memory_space=pltpu.VMEM)
    rows, width = terms[0].shape
    return pl.pallas_call(
        finish_kernel,
        out_shape=jax.ShapeDtypeStruct((rows, features), terms[0].dtype),
        in_specs=[vmem] * (1 + len(terms)),
        out_specs=vmem,
        compiler_params=pltpu.CompilerParams(vmem_limit_bytes=VMEM_LIMIT),
        cost_estimate=pl.CostEstimate(
            flops=rows * width * (len(terms) + 1),
            bytes_accessed=rows * width * 2 * (len(terms) + 2),
            transcendentals=0,
        ),
        name="finish",
    )(flag, *terms)


def body(
    queries,
    keys,
    values,
    sinks,
    segments,
    hidden_in,
    routes,
    w_out,
    norm_gain,
    router,
    w_gate_up,
    w_down,
):
    n_ctx = lax.axis_size("ctx")
    n_head = lax.axis_size("head")
    n_z = n_ctx // CORES
    ctx = lax.axis_index("ctx")
    head = lax.axis_index("head")
    tok_count = queries.shape[0]
    features = hidden_in.shape[1]
    experts = router.shape[1]
    own_rows = tok_count // n_head
    width = -(-(features + 2 * experts) // LANES) * LANES

    to_sibling = [(i, i ^ 1) for i in range(n_ctx)]
    ring = list(range(0, n_z, 2))
    ring = ring[::-1] + list(range(1, n_z, 2))
    follower = {ring[i]: ring[(i + 1) % n_z] for i in range(n_z)}
    to_next_chip = [(i, follower[i // CORES] * CORES + i % CORES) for i in range(n_ctx)]

    def sibling(x):
        return lax.ppermute(x, "ctx", to_sibling)

    def next_chip(x):
        return lax.ppermute(x, "ctx", to_next_chip)

    def next_head(x, j):
        return lax.ppermute(x, "head", [(i, (i + j) % n_head) for i in range(n_head)])

    def add(*terms):
        total = terms[0].astype(jnp.float32)
        for term in terms[1:]:
            total = total + term.astype(jnp.float32)
        return total.astype(jnp.bfloat16)

    def after(later, earlier):
        return lax.optimization_barrier((later, earlier))

    place = jnp.stack([ctx, head]).astype(jnp.int32)
    row_start = head * own_rows
    own_hidden = jnp.pad(
        lax.dynamic_slice_in_dim(hidden_in, row_start, own_rows, 0), ((0, 0), (0, width - features))
    )
    own_routes = lax.dynamic_slice_in_dim(routes, row_start, own_rows, 0)
    tok_seg = lax.dynamic_slice_in_dim(segments, ctx * tok_count, tok_count, 0)[:, None]
    tail = features - (width - LANES)
    router_lanes = jnp.pad(
        jnp.concatenate([router.T, router.T]), ((tail, LANES - tail - 2 * experts), (0, 0))
    )

    with jax.named_scope("keys_and_values"):
        own = side_by_side(keys, values)
        kv = [own] + [
            lax.ppermute(own, "ctx", [(i, i + CORES * k) for i in range(n_ctx - CORES * k)])
            for k in range(1, n_z)
        ]
    with jax.named_scope("attention"):
        q, bias = prepare(place, queries, tok_seg, segments[None, :])
        kv, q = after(kv, q)
        kv = [x for one in kv for x in (one, sibling(one))]
        sums = attend(place, sinks, q, bias, w_out.T, kv, n_head, width)

    with jax.named_scope("norm"):
        gathered = [sums[0]] + [next_head(sums[j], n_head - j) for j in range(1, n_head)]
        residual, rows = norm_and_gates(
            gathered, own_hidden, own_routes, norm_gain[None, :], router_lanes, experts
        )

    def to_heads(x):
        return [x] + [next_head(x, j) for j in range(1, n_head)]

    def to_other_heads(sums):
        return [next_head(sums[j - 1], n_head - j) for j in range(1, n_head)]

    with jax.named_scope("rows_of_chips"):
        near = to_heads(rows)
        chunk = next_chip(rows)
        down, gate_up_t, flag = load([w_down[0], jnp.swapaxes(w_gate_up[0], 1, 2)], rows)
        near, chunk, flag = lax.optimization_barrier((near, chunk, flag))

    waiting, arriving = None, []
    for hop in range(n_z):
        with jax.named_scope("rows_of_chips"):
            lot, coming = None, None
            if hop < n_z - 2 or hop == 0 and n_z > 1:
                lot = to_heads(chunk)
                coming = next_chip(chunk) if hop < n_z - 2 else None
            elif hop == n_z - 2:
                lot = [chunk] + [next_chip(x) for x in near[1:]]
        with jax.named_scope("experts"):
            far = [sibling(x) for x in near]
            *near_out, far_out, flag = expert_rows(
                place, near, far, gate_up_t, down, flag, experts
            )
        with jax.named_scope("sum_back"):
            lot, coming, waiting, arriving, far_out = lax.optimization_barrier(
                (lot, coming, waiting, arriving, far_out)
            )
            if waiting is not None:
                arriving = [next_chip(add(*waiting, *arriving))]
            crossed = sibling(far_out)
            blocks = [
                (near_out[j], crossed[j * own_rows : (j + 1) * own_rows]) for j in range(n_head)
            ]
            if hop == 0:
                own_blocks, before = blocks, far_out
            else:
                before = [add(*block) for block in blocks[1:]]
                waiting = [*blocks[0], *to_other_heads(before)]
            if lot is not None:
                near, before = after(lot, before)
                chunk = coming

    with jax.named_scope("sum_back"):
        if n_z > 1:
            waiting, own_blocks = after(waiting, own_blocks)
            arriving = [next_chip(add(*waiting, *arriving))]
        own_sums = to_other_heads([add(*block) for block in own_blocks[1:]])
        return finish(flag, [*own_blocks[0], residual, *own_sums, *arriving], features)


def solution(mesh):
    placed = (
        P(("group", "ctx"), "head"),
        P(("group", "ctx"), "head"),
        P(("group", "ctx"), "head"),
        P("head"),
        P("group"),
        P(("group", "ctx"), None),
        P(("group", "ctx"), None),
        P("head", None),
        P(),
        P(),
        P("ctx", None, None, "head"),
        P("ctx", "head", None),
    )
    return jax.shard_map(
        body,
        mesh=mesh,
        in_specs=placed,
        out_specs=P(("group", "ctx", "head"), None),
        check_vma=False,
    )
```

```python
import functools

import jax
import jax.numpy as jnp
from jax import lax
from jax.experimental import pallas as pl
from jax.experimental.pallas import tpu as pltpu
from jax.sharding import PartitionSpec as P

HEAD_SIZE = 64
LANES = 128
CORES = 2
VMEM_LIMIT = 16 << 20
STACKED_HEADS = 4
UNITS = 4 * LANES
COLUMNS = 6 * LANES

masked_value = -1e30
NT = (((1,), (1,)), ((), ()))
NN = (((1,), (0,)), ((), ()))


def dot(a, b, dims):
    return lax.dot_general(a, b, dims, preferred_element_type=jnp.float32)


def load_kernel(n, *refs):
    sources, targets, flag, arrived = refs[:n], refs[-n - 2 : -2], refs[-2], refs[-1]
    flag[...] = jnp.zeros(flag.shape, flag.dtype)
    copies = [pltpu.make_async_copy(sources[i], targets[i], arrived.at[i]) for i in range(n)]
    for copy in copies:
        copy.start()
    for copy in copies:
        copy.wait()


def load(arrays, earlier):
    n = len(arrays)
    return pl.pallas_call(
        functools.partial(load_kernel, n),
        out_shape=[pltpu.VMEM(a.shape, a.dtype) for a in arrays]
        + [jax.ShapeDtypeStruct((8, LANES), jnp.float32)],
        in_specs=[pl.BlockSpec(memory_space=pl.ANY)] * n
        + [pl.BlockSpec(memory_space=pltpu.VMEM)],
        out_specs=[pl.BlockSpec(memory_space=pltpu.VMEM)] * (n + 1),
        scratch_shapes=[pltpu.SemaphoreType.DMA((n,))],
        compiler_params=pltpu.CompilerParams(vmem_limit_bytes=VMEM_LIMIT),
        cost_estimate=pl.CostEstimate(
            flops=0, bytes_accessed=sum(4 * a.size for a in arrays), transcendentals=0
        ),
        name="load",
    )(*[in_hbm(a) for a in arrays], earlier)


def in_hbm(x):
    return pltpu.with_memory_space_constraint(x, pltpu.HBM)


def in_vmem(x):
    return pltpu.with_memory_space_constraint(x, pltpu.VMEM)


def pack_kernel(left, right, both, arrived):
    half = left.shape[1]
    if half % LANES:
        both[:, :half] = left[...]
        both[:, half:] = right[...]
        return
    copies = [
        pltpu.make_async_copy(left, both.at[:, pl.ds(0, half)], arrived.at[0]),
        pltpu.make_async_copy(right, both.at[:, pl.ds(half, half)], arrived.at[1]),
    ]
    for copy in copies:
        copy.start()
    for copy in copies:
        copy.wait()


def side_by_side(left, right):
    rows, half = left.shape
    vmem = pl.BlockSpec(memory_space=pltpu.VMEM)
    source = vmem if half % LANES else pl.BlockSpec(memory_space=pl.ANY)
    return pl.pallas_call(
        pack_kernel,
        out_shape=jax.ShapeDtypeStruct((rows, 2 * half), left.dtype),
        in_specs=[source] * 2,
        out_specs=vmem,
        scratch_shapes=[pltpu.SemaphoreType.DMA((2,))],
        compiler_params=pltpu.CompilerParams(vmem_limit_bytes=VMEM_LIMIT),
        cost_estimate=pl.CostEstimate(
            flops=0, bytes_accessed=8 * rows * half, transcendentals=0
        ),
        name="side_by_side",
    )(*[x if half % LANES else in_hbm(x) for x in (left, right)])


def prepare_kernel(place, q_ref, tok_seg, segments, q_out, bias):
    tok_count = q_ref.shape[0]
    for h in range(q_ref.shape[1] // HEAD_SIZE):
        q_out[h * tok_count : (h + 1) * tok_count, :] = q_ref[
            :, h * HEAD_SIZE : (h + 1) * HEAD_SIZE
        ] * jnp.asarray(HEAD_SIZE**-0.5, q_ref.dtype)
    ctx = place[0]
    z_here = ctx // CORES
    core = ctx - z_here * CORES
    first = jnp.sum((segments[...] < tok_seg[...]).astype(jnp.float32), axis=1, keepdims=True)
    tok = ctx * tok_count + lax.broadcasted_iota(jnp.int32, bias.shape, 0)
    lane = lax.broadcasted_iota(jnp.int32, bias.shape, 1)
    block = lane // tok_count
    hop = block // CORES
    owner = (z_here - hop) * CORES + jnp.where(block == hop * CORES, core, 1 - core)
    pos = owner * tok_count + (lane - block * tok_count)
    seen = (z_here >= hop) & (pos <= tok) & (pos.astype(jnp.float32) >= first)
    bias[...] = jnp.where(seen, 0.0, masked_value)


def prepare(place, q, tok_seg, segments):
    tok_count, columns = q.shape
    vmem = pl.BlockSpec(memory_space=pltpu.VMEM)
    return pl.pallas_call(
        prepare_kernel,
        out_shape=[
            jax.ShapeDtypeStruct((columns // HEAD_SIZE * tok_count, HEAD_SIZE), q.dtype),
            jax.ShapeDtypeStruct((tok_count, segments.shape[1]), jnp.float32),
        ],
        in_specs=[pl.BlockSpec(memory_space=pltpu.SMEM)] + [vmem] * 3,
        out_specs=[vmem] * 2,
        compiler_params=pltpu.CompilerParams(vmem_limit_bytes=VMEM_LIMIT),
        cost_estimate=pl.CostEstimate(
            flops=20 * tok_count * segments.shape[1],
            bytes_accessed=4 * tok_count * segments.shape[1],
            transcendentals=0,
        ),
        name="prepare",
    )(place, q, tok_seg, segments)


def attend_kernel(n_ctx, n_head, place, sinks, q_ref, bias, w_ref, *rest):
    kv_refs, rest = rest[:n_ctx], rest[n_ctx:]
    outs, (probs, attended, ordered, weights, arrived) = rest[:n_head], rest[n_head:]
    features = weights.shape[0]
    blocks = [(i, min(features, i + COLUMNS)) for i in range(0, features, COLUMNS)]
    copies = [
        pltpu.make_async_copy(
            w_ref.at[pl.ds(i, end - i)], weights.at[pl.ds(i, end - i)], arrived.at[n]
        )
        for n, (i, end) in enumerate(blocks)
    ]
    for copy in copies:
        copy.start()
    tok_count = bias.shape[0]
    own_rows = tok_count // n_head
    kv_width = kv_refs[0].shape[1] // 2
    kv_groups = kv_width // HEAD_SIZE
    share = q_ref.shape[0] // tok_count // kv_groups
    stack = min(share, STACKED_HEADS)
    for g in range(kv_groups):
        ks = slice(g * HEAD_SIZE, (g + 1) * HEAD_SIZE)
        vs = slice(kv_width + g * HEAD_SIZE, kv_width + (g + 1) * HEAD_SIZE)
        k = jnp.concatenate([ref[:, ks] for ref in kv_refs])
        v = jnp.concatenate([ref[:, vs] for ref in kv_refs])
        for j in range(0, share, stack):
            heads = range(g * share + j, g * share + min(share, j + stack))
            scores = dot(q_ref[heads[0] * tok_count : (heads[-1] + 1) * tok_count, :], k, NT)
            denoms = []
            for i, h in enumerate(heads):
                score = scores[i * tok_count : (i + 1) * tok_count] + bias[...]
                top = jnp.maximum(jnp.max(score, axis=1, keepdims=True), sinks[h])
                prob = jnp.exp(score - top)
                denoms.append(jnp.sum(prob, axis=1, keepdims=True) + jnp.exp(sinks[h] - top))
                probs[(j + i) * tok_count : (j + i + 1) * tok_count, :] = prob.astype(jnp.bfloat16)
            out = dot(probs[j * tok_count : (j + len(heads)) * tok_count, :], v, NN)
            for i, h in enumerate(heads):
                attended[:, h * HEAD_SIZE : (h + 1) * HEAD_SIZE] = (
                    out[i * tok_count : (i + 1) * tok_count] / denoms[i]
                ).astype(jnp.bfloat16)
    head = place[1]
    for j in range(n_head):
        source = lax.rem(head + n_head - j, n_head) * own_rows
        ordered[j * own_rows : (j + 1) * own_rows, :] = attended[
            pl.ds(pl.multiple_of(source, own_rows), own_rows), :
        ]
    width = outs[0].shape[1]
    for out in outs:
        out[:, width - LANES :] = jnp.zeros((own_rows, LANES), out.dtype)
    for copy, (i, end) in zip(copies, blocks):
        copy.wait()
        part = dot(ordered[...], weights[i:end, :], NT).astype(jnp.bfloat16)
        for j in range(n_head):
            outs[j][:, i:end] = part[j * own_rows : (j + 1) * own_rows]


def attend(place, sinks, q, bias, w_out_t, kv, n_head, width):
    tok_count, n_keys = bias.shape
    features, columns = w_out_t.shape
    own_rows = tok_count // n_head
    vmem = pl.BlockSpec(memory_space=pltpu.VMEM)
    smem = pl.BlockSpec(memory_space=pltpu.SMEM)
    share = columns // (kv[0].shape[1] // 2)
    return pl.pallas_call(
        functools.partial(attend_kernel, len(kv), n_head),
        out_shape=[jax.ShapeDtypeStruct((own_rows, width), jnp.bfloat16)] * n_head,
        in_specs=[smem, smem, vmem, vmem, pl.BlockSpec(memory_space=pl.ANY)] + [vmem] * len(kv),
        out_specs=[vmem] * n_head,
        scratch_shapes=[
            pltpu.VMEM((share * tok_count, n_keys), jnp.bfloat16),
            pltpu.VMEM((tok_count, columns), jnp.bfloat16),
            pltpu.VMEM((tok_count, columns), jnp.bfloat16),
            pltpu.VMEM(w_out_t.shape, w_out_t.dtype),
            pltpu.SemaphoreType.DMA((-(-features // COLUMNS),)),
        ],
        compiler_params=pltpu.CompilerParams(vmem_limit_bytes=2 * VMEM_LIMIT),
        cost_estimate=pl.CostEstimate(
            flops=4 * tok_count * columns * n_keys + 2 * tok_count * columns * features,
            bytes_accessed=2 * columns * features,
            transcendentals=tok_count * n_keys * columns // HEAD_SIZE,
        ),
        name="attend",
    )(place, sinks, q, bias, in_hbm(w_out_t), *kv)


def norm_kernel(experts, hidden, routes, gain, router, *refs):
    sums, (residual_out, rows_out) = refs[:-2], refs[-2:]
    features = gain.shape[1]
    total = sums[0][...].astype(jnp.float32)
    for other in sums[1:]:
        total = total + other[...].astype(jnp.float32)
    residual = (hidden[...].astype(jnp.float32) + total).astype(jnp.bfloat16)
    residual_out[...] = residual
    widened = residual[:, :features].astype(jnp.float32)
    scale_rows = lax.rsqrt(jnp.mean(widened * widened, axis=-1, keepdims=True) + 1e-05)
    normed = (widened * scale_rows * gain[...]).astype(jnp.bfloat16)
    logits = dot(normed, router[...], NT)
    tail = rows_out.shape[1] - LANES
    offset = features - tail
    lane = lax.broadcasted_iota(jnp.int32, logits.shape, 1)
    expert = lane - offset
    expert = jnp.where(expert >= experts, expert - experts, expert)
    named = routes[:, 0:1] == expert
    for k in range(1, routes.shape[1]):
        named = named | (routes[:, k : k + 1] == expert)
    high_lanes = (lane >= offset) & (lane < offset + experts)
    low_lanes = (lane >= offset + experts) & (lane < offset + 2 * experts)
    chosen = jnp.where(named & (high_lanes | low_lanes), logits, masked_value)
    top = jnp.max(chosen, axis=1, keepdims=True)
    weight = jnp.exp(chosen - top)
    denom = jnp.sum(jnp.where(high_lanes, weight, 0.0), axis=1, keepdims=True)
    gates = weight / denom
    high = gates.astype(jnp.bfloat16).astype(jnp.float32)
    packed = jnp.where(high_lanes, high, jnp.where(low_lanes, gates - high, 0.0))
    rows_out[:, :features] = normed
    end = rows_out[:, tail:].astype(jnp.float32)
    rows_out[:, tail:] = jnp.where(lane < offset, end, packed).astype(jnp.bfloat16)


def norm_and_gates(sums, hidden, routes, gain, router_lanes, experts):
    rows, width = hidden.shape
    features = gain.shape[1]
    vmem = pl.BlockSpec(memory_space=pltpu.VMEM)
    return pl.pallas_call(
        functools.partial(norm_kernel, experts),
        out_shape=[jax.ShapeDtypeStruct((rows, width), jnp.bfloat16)] * 2,
        in_specs=[vmem] * (4 + len(sums)),
        out_specs=[vmem] * 2,
        compiler_params=pltpu.CompilerParams(vmem_limit_bytes=VMEM_LIMIT),
        cost_estimate=pl.CostEstimate(
            flops=rows * features * LANES * 2,
            bytes_accessed=rows * features * 10,
            transcendentals=rows * LANES,
        ),
        name="norm_and_gates",
    )(hidden, routes, gain, router_lanes, *sums)


def expert_kernel(experts, n_head, place, gate_up, down, flag, *refs):
    near, far = refs[:n_head], refs[n_head : 2 * n_head]
    outs, (far_out, done, rows, hidden) = refs[2 * n_head : -4], refs[-4:]
    done[...] = flag[...]
    units, features = down.shape
    count, width = near[0].shape
    tail = width - LANES
    lane = lax.broadcasted_iota(jnp.int32, (count, LANES), 1) - (features - tail)
    mine = (lane == place[0]) | (lane == place[0] + experts)
    gates = []
    for i, ref in enumerate(near + far):
        rows[i * count : (i + 1) * count, :] = ref[:, :features]
        packed = ref[:, tail:].astype(jnp.float32)
        gates.append(jnp.sum(jnp.where(mine, packed, 0.0), axis=1, keepdims=True))
    for ref in (*outs, far_out):
        ref[:, tail:] = jnp.zeros((ref.shape[0], LANES), ref.dtype)
    for i in range(0, units, UNITS):
        end = min(units, i + UNITS)
        gate_pre = dot(rows[...], gate_up[0, i:end, :], NT)
        up_pre = dot(rows[...], gate_up[1, i:end, :], NT)
        act = gate_pre * jax.nn.sigmoid(1.702 * gate_pre) * (up_pre + 1.0)
        hidden[:, i:end] = act.astype(jnp.bfloat16)
    for i in range(0, features, COLUMNS):
        end = min(features, i + COLUMNS)
        part = dot(hidden[...], down[:, i:end], NN)
        for j in range(2 * n_head):
            block = (part[j * count : (j + 1) * count] * gates[j]).astype(jnp.bfloat16)
            if j < n_head:
                outs[j][:, i:end] = block
            else:
                far_out[(j - n_head) * count : (j - n_head + 1) * count, i:end] = block


def expert_rows(
                place, near, far, gate_up_t, down, flag, experts
            ):
    count, width = near[0].shape
    units, features = down.shape
    n_head = len(near)
    vmem = pl.BlockSpec(memory_space=pltpu.VMEM)
    return pl.pallas_call(
        functools.partial(expert_kernel, experts, n_head),
        out_shape=[jax.ShapeDtypeStruct((count, width), jnp.bfloat16)] * n_head
        + [jax.ShapeDtypeStruct((n_head * count, width), jnp.bfloat16)]
        + [jax.ShapeDtypeStruct(flag.shape, flag.dtype)],
        in_specs=[pl.BlockSpec(memory_space=pltpu.SMEM)] + [vmem] * (3 + 2 * n_head),
        out_specs=[vmem] * (n_head + 2),
        scratch_shapes=[
            pltpu.VMEM((2 * n_head * count, features), jnp.bfloat16),
            pltpu.VMEM((2 * n_head * count, units), jnp.bfloat16),
        ],
        compiler_params=pltpu.CompilerParams(vmem_limit_bytes=VMEM_LIMIT),
        cost_estimate=pl.CostEstimate(
            flops=12 * n_head * count * units * features,
            bytes_accessed=6 * units * features,
            transcendentals=2 * n_head * count * units,
        ),
        name="expert_rows",
    )(place, in_vmem(gate_up_t), in_vmem(down), flag, *near, *far)


def finish_kernel(n_halves, flag, *refs):
    terms, halves, out = refs[: len(refs) - 1 - n_halves], refs[len(refs) - 1 - n_halves : -1], refs[-1]
    features = out.shape[1]
    start = 0
    for half in halves or terms[:1]:
        end = min(features, start + half.shape[1])
        total = half[:, : end - start].astype(jnp.float32)
        for term in terms if halves else terms[1:]:
            total = total + term[:, start:end].astype(jnp.float32)
        out[:, start:end] = total.astype(out.dtype)
        start = end


def finish(flag, terms, halves, features):
    vmem = pl.BlockSpec(memory_space=pltpu.VMEM)
    rows, width = terms[0].shape
    return pl.pallas_call(
        functools.partial(finish_kernel, len(halves)),
        out_shape=jax.ShapeDtypeStruct((rows, features), terms[0].dtype),
        in_specs=[vmem] * (1 + len(terms) + len(halves)),
        out_specs=vmem,
        compiler_params=pltpu.CompilerParams(vmem_limit_bytes=VMEM_LIMIT),
        cost_estimate=pl.CostEstimate(
            flops=rows * width * (len(terms) + 1),
            bytes_accessed=rows * width * 2 * (len(terms) + 2),
            transcendentals=0,
        ),
        name="finish",
    )(flag, *terms, *halves)


def body(
    queries,
    keys,
    values,
    sinks,
    segments,
    hidden_in,
    routes,
    w_out,
    norm_gain,
    router,
    w_gate_up,
    w_down,
):
    n_ctx = lax.axis_size("ctx")
    n_head = lax.axis_size("head")
    n_z = n_ctx // CORES
    ctx = lax.axis_index("ctx")
    head = lax.axis_index("head")
    tok_count = queries.shape[0]
    features = hidden_in.shape[1]
    experts = router.shape[1]
    own_rows = tok_count // n_head
    width = -(-(features + 2 * experts) // LANES) * LANES

    to_sibling = [(i, i ^ 1) for i in range(n_ctx)]
    ring = list(range(0, n_z, 2))
    ring = ring[::-1] + list(range(1, n_z, 2))
    follower = {ring[i]: ring[(i + 1) % n_z] for i in range(n_z)}
    to_next_chip = [(i, follower[i // CORES] * CORES + i % CORES) for i in range(n_ctx)]

    def sibling(x):
        return lax.ppermute(x, "ctx", to_sibling)

    def next_chip(x):
        return lax.ppermute(x, "ctx", to_next_chip)

    def next_head(x, j):
        return lax.ppermute(x, "head", [(i, (i + j) % n_head) for i in range(n_head)])

    def add(*terms):
        total = terms[0].astype(jnp.float32)
        for term in terms[1:]:
            total = total + term.astype(jnp.float32)
        return total.astype(jnp.bfloat16)

    def after(later, earlier):
        return lax.optimization_barrier((later, earlier))

    place = jnp.stack([ctx, head]).astype(jnp.int32)
    row_start = head * own_rows
    own_hidden = jnp.pad(
        lax.dynamic_slice_in_dim(hidden_in, row_start, own_rows, 0), ((0, 0), (0, width - features))
    )
    own_routes = lax.dynamic_slice_in_dim(routes, row_start, own_rows, 0)
    tok_seg = lax.dynamic_slice_in_dim(segments, ctx * tok_count, tok_count, 0)[:, None]
    tail = features - (width - LANES)
    router_lanes = jnp.pad(
        jnp.concatenate([router.T, router.T]), ((tail, LANES - tail - 2 * experts), (0, 0))
    )

    with jax.named_scope("keys_and_values"):
        own = side_by_side(keys, values)
        kv = [
            lax.ppermute(own, "ctx", [(i, i + CORES * k) for i in range(n_ctx - CORES * k)])
            for k in range(n_z - 1, 0, -1)
        ]
        kv = [own] + kv[::-1]
    with jax.named_scope("attention"):
        q, bias = prepare(place, queries, tok_seg, segments[None, :])
        kv, q = after(kv, q)
        kv = [x for one in kv for x in (one, sibling(one))]
        sums = attend(place, sinks, q, bias, w_out.T, kv, n_head, width)

    with jax.named_scope("norm"):
        gathered = [sums[0]] + [next_head(sums[j], n_head - j) for j in range(1, n_head)]
        down, gate_up_t, flag = load([w_down[0], jnp.swapaxes(w_gate_up[0], 1, 2)], sums[0])
        gathered, flag = after(gathered, flag)
        residual, rows = norm_and_gates(
            gathered, own_hidden, own_routes, norm_gain[None, :], router_lanes, experts
        )

    def to_heads(x):
        return [x] + [next_head(x, j) for j in range(1, n_head)]

    def to_other_heads(sums):
        return [next_head(sums[j - 1], n_head - j) for j in range(1, n_head)]

    with jax.named_scope("rows_of_chips"):
        near = to_heads(rows)
        chunk = next_chip(rows)
        near, chunk, flag = lax.optimization_barrier((near, chunk, flag))

    middle = -(-width // LANES // 2) * LANES
    halves = [slice(0, middle), slice(middle, width)]
    waiting, arriving = None, []
    for hop in range(n_z):
        with jax.named_scope("rows_of_chips"):
            lot, coming = None, None
            if hop < n_z - 2 or hop == 0 and n_z > 1:
                lot = to_heads(chunk)
                coming = next_chip(chunk) if hop < n_z - 2 else None
            elif hop == n_z - 2:
                lot = [chunk] + [next_chip(x) for x in near[1:]]
        with jax.named_scope("experts"):
            far = [sibling(x) for x in near]
            *near_out, far_out, flag = expert_rows(
                place, near, far, gate_up_t, down, flag, experts
            )
        with jax.named_scope("sum_back"):
            lot, coming, waiting, arriving, far_out = lax.optimization_barrier(
                (lot, coming, waiting, arriving, far_out)
            )
            if waiting is not None:
                sent = halves if hop == n_z - 1 else [slice(0, width)]
                arriving = [
                    next_chip(add(*[x[:, part] for x in (*waiting, *arriving)])) for part in sent
                ]
            crossed = sibling(far_out)
            blocks = [
                (near_out[j], crossed[j * own_rows : (j + 1) * own_rows]) for j in range(n_head)
            ]
            if hop == 0:
                own_blocks = blocks
            elif hop < n_z - 1:
                leaving = [add(*block) for block in blocks[1:]]
                leaving, flag = after(leaving, flag)
                waiting = [*blocks[0], *to_other_heads(leaving)]
            near, chunk = lot, coming

    with jax.named_scope("sum_back"):
        if n_z > 1:
            others = [[add(*[x[:, half] for x in b]) for b in blocks[1:]] for half in halves]
            crossing = [to_other_heads(x) for x in others]
            crossing[0], own_blocks = after(crossing[0], own_blocks)
            arriving = [
                next_chip(
                    add(*[x[:, half] for x in blocks[0]], *crossing[i], *arriving[i : i + 1])
                )
                for i, half in enumerate(halves)
            ]
        own_sums = to_other_heads([add(*block) for block in own_blocks[1:]])
        return finish(flag, [*own_blocks[0], residual, *own_sums], arriving, features)


def solution(mesh):
    placed = (
        P(("group", "ctx"), "head"),
        P(("group", "ctx"), "head"),
        P(("group", "ctx"), "head"),
        P("head"),
        P("group"),
        P(("group", "ctx"), None),
        P(("group", "ctx"), None),
        P("head", None),
        P(),
        P(),
        P("ctx", None, None, "head"),
        P("ctx", "head", None),
    )
    return jax.shard_map(
        body,
        mesh=mesh,
        in_specs=placed,
        out_specs=P(("group", "ctx", "head"), None),
        check_vma=False,
    )
```

```python
import functools

import jax
import jax.numpy as jnp
from jax import lax
from jax.experimental import pallas as pl
from jax.experimental.pallas import tpu as pltpu
from jax.sharding import PartitionSpec as P

HEAD_SIZE = 64
LANES = 128
CORES = 2
VMEM_LIMIT = 16 << 20
STACKED_HEADS = 4
UNIT_PARTS = 3
BF16_ROWS = 16
COLUMNS = 6 * LANES

masked_value = -1e30
NT = (((1,), (1,)), ((), ()))
NN = (((1,), (0,)), ((), ()))


def dot(a, b, dims):
    return lax.dot_general(a, b, dims, preferred_element_type=jnp.float32)


def load_kernel(n, *refs):
    sources, targets, flag, arrived = refs[:n], refs[-n - 2 : -2], refs[-2], refs[-1]
    flag[...] = jnp.zeros(flag.shape, flag.dtype)
    copies = [pltpu.make_async_copy(sources[i], targets[i], arrived.at[i]) for i in range(n)]
    for copy in copies:
        copy.start()
    for copy in copies:
        copy.wait()


def load(arrays, earlier):
    n = len(arrays)
    return pl.pallas_call(
        functools.partial(load_kernel, n),
        out_shape=[pltpu.VMEM(a.shape, a.dtype) for a in arrays]
        + [jax.ShapeDtypeStruct((8, LANES), jnp.float32)],
        in_specs=[pl.BlockSpec(memory_space=pl.ANY)] * n
        + [pl.BlockSpec(memory_space=pltpu.VMEM)],
        out_specs=[pl.BlockSpec(memory_space=pltpu.VMEM)] * (n + 1),
        scratch_shapes=[pltpu.SemaphoreType.DMA((n,))],
        compiler_params=pltpu.CompilerParams(vmem_limit_bytes=VMEM_LIMIT),
        cost_estimate=pl.CostEstimate(
            flops=0, bytes_accessed=sum(4 * a.size for a in arrays), transcendentals=0
        ),
        name="load",
    )(*[in_hbm(a) for a in arrays], earlier)


def in_hbm(x):
    return pltpu.with_memory_space_constraint(x, pltpu.HBM)


def in_vmem(x):
    return pltpu.with_memory_space_constraint(x, pltpu.VMEM)


def pack_kernel(left, right, both, arrived):
    half = left.shape[1]
    if half % LANES:
        both[:, :half] = left[...]
        both[:, half:] = right[...]
        return
    copies = [
        pltpu.make_async_copy(left, both.at[:, pl.ds(0, half)], arrived.at[0]),
        pltpu.make_async_copy(right, both.at[:, pl.ds(half, half)], arrived.at[1]),
    ]
    for copy in copies:
        copy.start()
    for copy in copies:
        copy.wait()


def side_by_side(left, right):
    rows, half = left.shape
    vmem = pl.BlockSpec(memory_space=pltpu.VMEM)
    source = vmem if half % LANES else pl.BlockSpec(memory_space=pl.ANY)
    return pl.pallas_call(
        pack_kernel,
        out_shape=jax.ShapeDtypeStruct((rows, 2 * half), left.dtype),
        in_specs=[source] * 2,
        out_specs=vmem,
        scratch_shapes=[pltpu.SemaphoreType.DMA((2,))],
        compiler_params=pltpu.CompilerParams(vmem_limit_bytes=VMEM_LIMIT),
        cost_estimate=pl.CostEstimate(
            flops=0, bytes_accessed=8 * rows * half, transcendentals=0
        ),
        name="side_by_side",
    )(*[x if half % LANES else in_hbm(x) for x in (left, right)])


def prepare_kernel(place, q_ref, tok_seg, segments, q_out, bias):
    tok_count = q_ref.shape[0]
    for h in range(q_ref.shape[1] // HEAD_SIZE):
        q_out[h * tok_count : (h + 1) * tok_count, :] = q_ref[
            :, h * HEAD_SIZE : (h + 1) * HEAD_SIZE
        ] * jnp.asarray(HEAD_SIZE**-0.5, q_ref.dtype)
    ctx = place[0]
    z_here = ctx // CORES
    core = ctx - z_here * CORES
    first = jnp.sum((segments[...] < tok_seg[...]).astype(jnp.float32), axis=1, keepdims=True)
    tok = ctx * tok_count + lax.broadcasted_iota(jnp.int32, bias.shape, 0)
    lane = lax.broadcasted_iota(jnp.int32, bias.shape, 1)
    block = lane // tok_count
    hop = block // CORES
    owner = (z_here - hop) * CORES + jnp.where(block == hop * CORES, core, 1 - core)
    pos = owner * tok_count + (lane - block * tok_count)
    seen = (z_here >= hop) & (pos <= tok) & (pos.astype(jnp.float32) >= first)
    bias[...] = jnp.where(seen, 0.0, masked_value)


def prepare(place, q, tok_seg, segments):
    tok_count, columns = q.shape
    vmem = pl.BlockSpec(memory_space=pltpu.VMEM)
    return pl.pallas_call(
        prepare_kernel,
        out_shape=[
            jax.ShapeDtypeStruct((columns // HEAD_SIZE * tok_count, HEAD_SIZE), q.dtype),
            jax.ShapeDtypeStruct((tok_count, segments.shape[1]), jnp.float32),
        ],
        in_specs=[pl.BlockSpec(memory_space=pltpu.SMEM)] + [vmem] * 3,
        out_specs=[vmem] * 2,
        compiler_params=pltpu.CompilerParams(vmem_limit_bytes=VMEM_LIMIT),
        cost_estimate=pl.CostEstimate(
            flops=20 * tok_count * segments.shape[1],
            bytes_accessed=4 * tok_count * segments.shape[1],
            transcendentals=0,
        ),
        name="prepare",
    )(place, q, tok_seg, segments)


def attend_kernel(n_ctx, n_head, place, sinks, q_ref, bias, w_ref, *rest):
    kv_refs, rest = rest[:n_ctx], rest[n_ctx:]
    outs, (probs, attended, ordered, weights, arrived) = rest[:n_head], rest[n_head:]
    features = weights.shape[0]
    blocks = [(i, min(features, i + COLUMNS)) for i in range(0, features, COLUMNS)]
    copies = [
        pltpu.make_async_copy(
            w_ref.at[pl.ds(i, end - i)], weights.at[pl.ds(i, end - i)], arrived.at[n]
        )
        for n, (i, end) in enumerate(blocks)
    ]
    for copy in copies:
        copy.start()
    tok_count = bias.shape[0]
    own_rows = tok_count // n_head
    kv_width = kv_refs[0].shape[1] // 2
    kv_groups = kv_width // HEAD_SIZE
    share = q_ref.shape[0] // tok_count // kv_groups
    stack = min(share, STACKED_HEADS)
    for g in range(kv_groups):
        ks = slice(g * HEAD_SIZE, (g + 1) * HEAD_SIZE)
        vs = slice(kv_width + g * HEAD_SIZE, kv_width + (g + 1) * HEAD_SIZE)
        k = jnp.concatenate([ref[:, ks] for ref in kv_refs])
        v = jnp.concatenate([ref[:, vs] for ref in kv_refs])
        for j in range(0, share, stack):
            heads = range(g * share + j, g * share + min(share, j + stack))
            scores = dot(q_ref[heads[0] * tok_count : (heads[-1] + 1) * tok_count, :], k, NT)
            denoms = []
            for i, h in enumerate(heads):
                score = scores[i * tok_count : (i + 1) * tok_count] + bias[...]
                top = jnp.maximum(jnp.max(score, axis=1, keepdims=True), sinks[h])
                prob = jnp.exp(score - top)
                denoms.append(jnp.sum(prob, axis=1, keepdims=True) + jnp.exp(sinks[h] - top))
                probs[(j + i) * tok_count : (j + i + 1) * tok_count, :] = prob.astype(jnp.bfloat16)
            out = dot(probs[j * tok_count : (j + len(heads)) * tok_count, :], v, NN)
            for i, h in enumerate(heads):
                attended[:, h * HEAD_SIZE : (h + 1) * HEAD_SIZE] = (
                    out[i * tok_count : (i + 1) * tok_count] / denoms[i]
                ).astype(jnp.bfloat16)
    head = place[1]
    for j in range(n_head):
        source = lax.rem(head + n_head - j, n_head) * own_rows
        ordered[j * own_rows : (j + 1) * own_rows, :] = attended[
            pl.ds(pl.multiple_of(source, own_rows), own_rows), :
        ]
    width = outs[0].shape[1]
    for out in outs:
        out[:, width - LANES :] = jnp.zeros((own_rows, LANES), out.dtype)
    for copy, (i, end) in zip(copies, blocks):
        copy.wait()
        part = dot(ordered[...], weights[i:end, :], NT).astype(jnp.bfloat16)
        for j in range(n_head):
            outs[j][:, i:end] = part[j * own_rows : (j + 1) * own_rows]


def attend(place, sinks, q, bias, w_out_t, kv, n_head, width):
    tok_count, n_keys = bias.shape
    features, columns = w_out_t.shape
    own_rows = tok_count // n_head
    vmem = pl.BlockSpec(memory_space=pltpu.VMEM)
    smem = pl.BlockSpec(memory_space=pltpu.SMEM)
    share = columns // (kv[0].shape[1] // 2)
    return pl.pallas_call(
        functools.partial(attend_kernel, len(kv), n_head),
        out_shape=[jax.ShapeDtypeStruct((own_rows, width), jnp.bfloat16)] * n_head,
        in_specs=[smem, smem, vmem, vmem, pl.BlockSpec(memory_space=pl.ANY)] + [vmem] * len(kv),
        out_specs=[vmem] * n_head,
        scratch_shapes=[
            pltpu.VMEM((share * tok_count, n_keys), jnp.bfloat16),
            pltpu.VMEM((tok_count, columns), jnp.bfloat16),
            pltpu.VMEM((tok_count, columns), jnp.bfloat16),
            pltpu.VMEM(w_out_t.shape, w_out_t.dtype),
            pltpu.SemaphoreType.DMA((-(-features // COLUMNS),)),
        ],
        compiler_params=pltpu.CompilerParams(vmem_limit_bytes=2 * VMEM_LIMIT),
        cost_estimate=pl.CostEstimate(
            flops=4 * tok_count * columns * n_keys + 2 * tok_count * columns * features,
            bytes_accessed=2 * columns * features,
            transcendentals=tok_count * n_keys * columns // HEAD_SIZE,
        ),
        name="attend",
    )(place, sinks, q, bias, in_hbm(w_out_t), *kv)


def norm_kernel(experts, hidden, routes, gain, router, *refs):
    sums, (residual_out, rows_out) = refs[:-2], refs[-2:]
    features = gain.shape[1]
    total = sums[0][...].astype(jnp.float32)
    for other in sums[1:]:
        total = total + other[...].astype(jnp.float32)
    residual = (hidden[...].astype(jnp.float32) + total).astype(jnp.bfloat16)
    residual_out[...] = residual
    widened = residual[:, :features].astype(jnp.float32)
    scale_rows = lax.rsqrt(jnp.mean(widened * widened, axis=-1, keepdims=True) + 1e-05)
    normed = (widened * scale_rows * gain[...]).astype(jnp.bfloat16)
    logits = dot(normed, router[...], NT)
    tail = rows_out.shape[1] - LANES
    offset = features - tail
    lane = lax.broadcasted_iota(jnp.int32, logits.shape, 1)
    expert = lane - offset
    expert = jnp.where(expert >= experts, expert - experts, expert)
    named = routes[:, 0:1] == expert
    for k in range(1, routes.shape[1]):
        named = named | (routes[:, k : k + 1] == expert)
    high_lanes = (lane >= offset) & (lane < offset + experts)
    low_lanes = (lane >= offset + experts) & (lane < offset + 2 * experts)
    chosen = jnp.where(named & (high_lanes | low_lanes), logits, masked_value)
    top = jnp.max(chosen, axis=1, keepdims=True)
    weight = jnp.exp(chosen - top)
    denom = jnp.sum(jnp.where(high_lanes, weight, 0.0), axis=1, keepdims=True)
    gates = weight / denom
    high = gates.astype(jnp.bfloat16).astype(jnp.float32)
    packed = jnp.where(high_lanes, high, jnp.where(low_lanes, gates - high, 0.0))
    rows_out[:, :features] = normed
    end = rows_out[:, tail:].astype(jnp.float32)
    rows_out[:, tail:] = jnp.where(lane < offset, end, packed).astype(jnp.bfloat16)


def norm_and_gates(sums, hidden, routes, gain, router_lanes, experts):
    rows, width = hidden.shape
    features = gain.shape[1]
    vmem = pl.BlockSpec(memory_space=pltpu.VMEM)
    return pl.pallas_call(
        functools.partial(norm_kernel, experts),
        out_shape=[jax.ShapeDtypeStruct((rows, width), jnp.bfloat16)] * 2,
        in_specs=[vmem] * (4 + len(sums)),
        out_specs=[vmem] * 2,
        compiler_params=pltpu.CompilerParams(vmem_limit_bytes=VMEM_LIMIT),
        cost_estimate=pl.CostEstimate(
            flops=rows * features * LANES * 2,
            bytes_accessed=rows * features * 10,
            transcendentals=rows * LANES,
        ),
        name="norm_and_gates",
    )(hidden, routes, gain, router_lanes, *sums)


def expert_kernel(experts, n_head, place, gate_up, down, flag, *refs):
    near, far = refs[:n_head], refs[n_head : 2 * n_head]
    outs, (far_out, done, rows, hidden) = refs[2 * n_head : -4], refs[-4:]
    done[...] = flag[...]
    units, features = down.shape
    count, width = near[0].shape
    tail = width - LANES
    lane = lax.broadcasted_iota(jnp.int32, (count, LANES), 1) - (features - tail)
    mine = (lane == place[0]) | (lane == place[0] + experts)
    gates = []
    for i, ref in enumerate(near + far):
        rows[i * count : (i + 1) * count, :] = ref[:, :features]
        packed = ref[:, tail:].astype(jnp.float32)
        gates.append(jnp.sum(jnp.where(mine, packed, 0.0), axis=1, keepdims=True))
    for ref in (*outs, far_out):
        ref[:, tail:] = jnp.zeros((ref.shape[0], LANES), ref.dtype)
    parts, _, block = hidden.shape

    def some_units(n, carry):
        here = pl.ds(pl.multiple_of(n * block, BF16_ROWS), block) if parts > 1 else slice(None)
        gate_pre = dot(rows[...], gate_up[0, here, :], NT)
        up_pre = dot(rows[...], gate_up[1, here, :], NT)
        act = gate_pre * jax.nn.sigmoid(1.702 * gate_pre) * (up_pre + 1.0)
        hidden[n] = act.astype(jnp.bfloat16)
        return carry

    lax.fori_loop(0, parts, some_units, 0)
    units_by_row = jnp.concatenate([hidden[n] for n in range(parts)], axis=1)
    for i in range(0, features, COLUMNS):
        end = min(features, i + COLUMNS)
        part = dot(units_by_row, down[:, i:end], NN)
        for j in range(2 * n_head):
            block = (part[j * count : (j + 1) * count] * gates[j]).astype(jnp.bfloat16)
            if j < n_head:
                outs[j][:, i:end] = block
            else:
                far_out[(j - n_head) * count : (j - n_head + 1) * count, i:end] = block


def expert_rows(
                place, near, far, gate_up_t, down, flag, experts
            ):
    count, width = near[0].shape
    units, features = down.shape
    n_head = len(near)
    parts = UNIT_PARTS if units % (UNIT_PARTS * BF16_ROWS) == 0 else 1
    vmem = pl.BlockSpec(memory_space=pltpu.VMEM)
    return pl.pallas_call(
        functools.partial(expert_kernel, experts, n_head),
        out_shape=[jax.ShapeDtypeStruct((count, width), jnp.bfloat16)] * n_head
        + [jax.ShapeDtypeStruct((n_head * count, width), jnp.bfloat16)]
        + [jax.ShapeDtypeStruct(flag.shape, flag.dtype)],
        in_specs=[pl.BlockSpec(memory_space=pltpu.SMEM)] + [vmem] * (3 + 2 * n_head),
        out_specs=[vmem] * (n_head + 2),
        scratch_shapes=[
            pltpu.VMEM((2 * n_head * count, features), jnp.bfloat16),
            pltpu.VMEM((parts, 2 * n_head * count, units // parts), jnp.bfloat16),
        ],
        compiler_params=pltpu.CompilerParams(vmem_limit_bytes=VMEM_LIMIT),
        cost_estimate=pl.CostEstimate(
            flops=12 * n_head * count * units * features,
            bytes_accessed=6 * units * features,
            transcendentals=2 * n_head * count * units,
        ),
        name="expert_rows",
    )(place, in_vmem(gate_up_t), in_vmem(down), flag, *near, *far)


def finish_kernel(n_halves, flag, *refs):
    terms, halves, out = refs[: len(refs) - 1 - n_halves], refs[len(refs) - 1 - n_halves : -1], refs[-1]
    features = out.shape[1]
    start = 0
    for half in halves or terms[:1]:
        end = min(features, start + half.shape[1])
        total = half[:, : end - start].astype(jnp.float32)
        for term in terms if halves else terms[1:]:
            total = total + term[:, start:end].astype(jnp.float32)
        out[:, start:end] = total.astype(out.dtype)
        start = end


def finish(flag, terms, halves, features):
    vmem = pl.BlockSpec(memory_space=pltpu.VMEM)
    rows, width = terms[0].shape
    return pl.pallas_call(
        functools.partial(finish_kernel, len(halves)),
        out_shape=jax.ShapeDtypeStruct((rows, features), terms[0].dtype),
        in_specs=[vmem] * (1 + len(terms) + len(halves)),
        out_specs=vmem,
        compiler_params=pltpu.CompilerParams(vmem_limit_bytes=VMEM_LIMIT),
        cost_estimate=pl.CostEstimate(
            flops=rows * width * (len(terms) + 1),
            bytes_accessed=rows * width * 2 * (len(terms) + 2),
            transcendentals=0,
        ),
        name="finish",
    )(flag, *terms, *halves)


def body(
    queries,
    keys,
    values,
    sinks,
    segments,
    hidden_in,
    routes,
    w_out,
    norm_gain,
    router,
    w_gate_up,
    w_down,
):
    n_ctx = lax.axis_size("ctx")
    n_head = lax.axis_size("head")
    n_z = n_ctx // CORES
    ctx = lax.axis_index("ctx")
    head = lax.axis_index("head")
    tok_count = queries.shape[0]
    features = hidden_in.shape[1]
    experts = router.shape[1]
    own_rows = tok_count // n_head
    width = -(-(features + 2 * experts) // LANES) * LANES

    to_sibling = [(i, i ^ 1) for i in range(n_ctx)]
    ring = list(range(0, n_z, 2))
    ring = ring[::-1] + list(range(1, n_z, 2))
    follower = {ring[i]: ring[(i + 1) % n_z] for i in range(n_z)}
    to_next_chip = [(i, follower[i // CORES] * CORES + i % CORES) for i in range(n_ctx)]

    def sibling(x):
        return lax.ppermute(x, "ctx", to_sibling)

    def next_chip(x):
        return lax.ppermute(x, "ctx", to_next_chip)

    def next_head(x, j):
        return lax.ppermute(x, "head", [(i, (i + j) % n_head) for i in range(n_head)])

    def add(*terms):
        total = terms[0].astype(jnp.float32)
        for term in terms[1:]:
            total = total + term.astype(jnp.float32)
        return total.astype(jnp.bfloat16)

    def after(later, earlier):
        return lax.optimization_barrier((later, earlier))

    place = jnp.stack([ctx, head]).astype(jnp.int32)
    row_start = head * own_rows
    own_hidden = jnp.pad(
        lax.dynamic_slice_in_dim(hidden_in, row_start, own_rows, 0), ((0, 0), (0, width - features))
    )
    own_routes = lax.dynamic_slice_in_dim(routes, row_start, own_rows, 0)
    tok_seg = lax.dynamic_slice_in_dim(segments, ctx * tok_count, tok_count, 0)[:, None]
    tail = features - (width - LANES)
    router_lanes = jnp.pad(
        jnp.concatenate([router.T, router.T]), ((tail, LANES - tail - 2 * experts), (0, 0))
    )

    with jax.named_scope("keys_and_values"):
        own = side_by_side(keys, values)
        kv = [
            lax.ppermute(own, "ctx", [(i, i + CORES * k) for i in range(n_ctx - CORES * k)])
            for k in range(n_z - 1, 0, -1)
        ]
        kv = [own] + kv[::-1]
    with jax.named_scope("attention"):
        q, bias = prepare(place, queries, tok_seg, segments[None, :])
        kv, q = after(kv, q)
        kv = [x for one in kv for x in (one, sibling(one))]
        sums = attend(place, sinks, q, bias, w_out.T, kv, n_head, width)

    with jax.named_scope("norm"):
        gathered = [sums[0]] + [next_head(sums[j], n_head - j) for j in range(1, n_head)]
        down, gate_up_t, flag = load([w_down[0], jnp.swapaxes(w_gate_up[0], 1, 2)], sums[0])
        gathered, flag = after(gathered, flag)
        residual, rows = norm_and_gates(
            gathered, own_hidden, own_routes, norm_gain[None, :], router_lanes, experts
        )

    def to_heads(x):
        return [x] + [next_head(x, j) for j in range(1, n_head)]

    def to_other_heads(sums):
        return [next_head(sums[j - 1], n_head - j) for j in range(1, n_head)]

    with jax.named_scope("rows_of_chips"):
        near = to_heads(rows)
        chunk = next_chip(rows)
        near, chunk, flag = lax.optimization_barrier((near, chunk, flag))

    middle = -(-width // LANES // 2) * LANES
    halves = [slice(0, middle), slice(middle, width)]
    waiting, arriving = None, []
    for hop in range(n_z):
        with jax.named_scope("rows_of_chips"):
            lot, coming = None, None
            if hop < n_z - 2 or hop == 0 and n_z > 1:
                lot = to_heads(chunk)
                coming = next_chip(chunk) if hop < n_z - 2 else None
            elif hop == n_z - 2:
                lot = [chunk] + [next_chip(x) for x in near[1:]]
        with jax.named_scope("experts"):
            far = [sibling(x) for x in near]
            *near_out, far_out, flag = expert_rows(
                place, near, far, gate_up_t, down, flag, experts
            )
        with jax.named_scope("sum_back"):
            lot, coming, waiting, arriving, far_out = lax.optimization_barrier(
                (lot, coming, waiting, arriving, far_out)
            )
            if waiting is not None:
                sent = halves if hop == n_z - 1 else [slice(0, width)]
                arriving = [
                    next_chip(add(*[x[:, part] for x in (*waiting, *arriving)])) for part in sent
                ]
            crossed = sibling(far_out)
            blocks = [
                (near_out[j], crossed[j * own_rows : (j + 1) * own_rows]) for j in range(n_head)
            ]
            if hop == 0:
                own_blocks = blocks
            elif hop < n_z - 1:
                leaving = [add(*block) for block in blocks[1:]]
                leaving, flag = after(leaving, flag)
                waiting = [*blocks[0], *to_other_heads(leaving)]
            near, chunk = lot, coming

    with jax.named_scope("sum_back"):
        if n_z > 1:
            others = [[add(*[x[:, half] for x in b]) for b in blocks[1:]] for half in halves]
            crossing = [to_other_heads(x) for x in others]
            crossing[0], own_blocks = after(crossing[0], own_blocks)
            arriving = [
                next_chip(
                    add(*[x[:, half] for x in blocks[0]], *crossing[i], *arriving[i : i + 1])
                )
                for i, half in enumerate(halves)
            ]
        own_sums = to_other_heads([add(*block) for block in own_blocks[1:]])
        return finish(flag, [*own_blocks[0], residual, *own_sums], arriving, features)


def solution(mesh):
    placed = (
        P(("group", "ctx"), "head"),
        P(("group", "ctx"), "head"),
        P(("group", "ctx"), "head"),
        P("head"),
        P("group"),
        P(("group", "ctx"), None),
        P(("group", "ctx"), None),
        P("head", None),
        P(),
        P(),
        P("ctx", None, None, "head"),
        P("ctx", "head", None),
    )
    return jax.shard_map(
        body,
        mesh=mesh,
        in_specs=placed,
        out_specs=P(("group", "ctx", "head"), None),
        check_vma=False,
    )
```

```python
import functools

import jax
import jax.numpy as jnp
from jax import lax
from jax.experimental import pallas as pl
from jax.experimental.pallas import tpu as pltpu
from jax.sharding import PartitionSpec as P

HEAD_SIZE = 64
LANES = 128
CORES = 2
VMEM_LIMIT = 16 << 20
STACKED_HEADS = 4
UNIT_PARTS = 2
BF16_ROWS = 16
COLUMNS = 12 * LANES

masked_value = -1e30
NT = (((1,), (1,)), ((), ()))
NN = (((1,), (0,)), ((), ()))


def dot(a, b, dims):
    return lax.dot_general(a, b, dims, preferred_element_type=jnp.float32)


def load_kernel(n, *refs):
    sources, targets, flag, arrived = refs[:n], refs[-n - 2 : -2], refs[-2], refs[-1]
    flag[...] = jnp.zeros(flag.shape, flag.dtype)
    copies = [pltpu.make_async_copy(sources[i], targets[i], arrived.at[i]) for i in range(n)]
    for copy in copies:
        copy.start()
    for copy in copies:
        copy.wait()


def load(arrays, earlier):
    n = len(arrays)
    return pl.pallas_call(
        functools.partial(load_kernel, n),
        out_shape=[pltpu.VMEM(a.shape, a.dtype) for a in arrays]
        + [jax.ShapeDtypeStruct((8, LANES), jnp.float32)],
        in_specs=[pl.BlockSpec(memory_space=pl.ANY)] * n
        + [pl.BlockSpec(memory_space=pltpu.VMEM)],
        out_specs=[pl.BlockSpec(memory_space=pltpu.VMEM)] * (n + 1),
        scratch_shapes=[pltpu.SemaphoreType.DMA((n,))],
        compiler_params=pltpu.CompilerParams(vmem_limit_bytes=VMEM_LIMIT),
        cost_estimate=pl.CostEstimate(
            flops=0, bytes_accessed=sum(4 * a.size for a in arrays), transcendentals=0
        ),
        name="load",
    )(*[in_hbm(a) for a in arrays], earlier)


def in_hbm(x):
    return pltpu.with_memory_space_constraint(x, pltpu.HBM)


def in_vmem(x):
    return pltpu.with_memory_space_constraint(x, pltpu.VMEM)


def pack_kernel(left, right, both, arrived):
    half = left.shape[1]
    if half % LANES:
        both[:, :half] = left[...]
        both[:, half:] = right[...]
        return
    copies = [
        pltpu.make_async_copy(left, both.at[:, pl.ds(0, half)], arrived.at[0]),
        pltpu.make_async_copy(right, both.at[:, pl.ds(half, half)], arrived.at[1]),
    ]
    for copy in copies:
        copy.start()
    for copy in copies:
        copy.wait()


def side_by_side(left, right):
    rows, half = left.shape
    vmem = pl.BlockSpec(memory_space=pltpu.VMEM)
    source = vmem if half % LANES else pl.BlockSpec(memory_space=pl.ANY)
    return pl.pallas_call(
        pack_kernel,
        out_shape=jax.ShapeDtypeStruct((rows, 2 * half), left.dtype),
        in_specs=[source] * 2,
        out_specs=vmem,
        scratch_shapes=[pltpu.SemaphoreType.DMA((2,))],
        compiler_params=pltpu.CompilerParams(vmem_limit_bytes=VMEM_LIMIT),
        cost_estimate=pl.CostEstimate(
            flops=0, bytes_accessed=8 * rows * half, transcendentals=0
        ),
        name="side_by_side",
    )(*[x if half % LANES else in_hbm(x) for x in (left, right)])


def prepare_kernel(place, q_ref, tok_seg, segments, q_out, bias):
    tok_count = q_ref.shape[0]
    for h in range(q_ref.shape[1] // HEAD_SIZE):
        q_out[h * tok_count : (h + 1) * tok_count, :] = q_ref[
            :, h * HEAD_SIZE : (h + 1) * HEAD_SIZE
        ] * jnp.asarray(HEAD_SIZE**-0.5, q_ref.dtype)
    ctx = place[0]
    z_here = ctx // CORES
    core = ctx - z_here * CORES
    first = jnp.sum((segments[...] < tok_seg[...]).astype(jnp.float32), axis=1, keepdims=True)
    tok = ctx * tok_count + lax.broadcasted_iota(jnp.int32, bias.shape, 0)
    lane = lax.broadcasted_iota(jnp.int32, bias.shape, 1)
    block = lane // tok_count
    hop = block // CORES
    owner = (z_here - hop) * CORES + jnp.where(block == hop * CORES, core, 1 - core)
    pos = owner * tok_count + (lane - block * tok_count)
    seen = (z_here >= hop) & (pos <= tok) & (pos.astype(jnp.float32) >= first)
    bias[...] = jnp.where(seen, 0.0, masked_value)


def prepare(place, q, tok_seg, segments):
    tok_count, columns = q.shape
    vmem = pl.BlockSpec(memory_space=pltpu.VMEM)
    return pl.pallas_call(
        prepare_kernel,
        out_shape=[
            jax.ShapeDtypeStruct((columns // HEAD_SIZE * tok_count, HEAD_SIZE), q.dtype),
            jax.ShapeDtypeStruct((tok_count, segments.shape[1]), jnp.float32),
        ],
        in_specs=[pl.BlockSpec(memory_space=pltpu.SMEM)] + [vmem] * 3,
        out_specs=[vmem] * 2,
        compiler_params=pltpu.CompilerParams(vmem_limit_bytes=VMEM_LIMIT),
        cost_estimate=pl.CostEstimate(
            flops=20 * tok_count * segments.shape[1],
            bytes_accessed=4 * tok_count * segments.shape[1],
            transcendentals=0,
        ),
        name="prepare",
    )(place, q, tok_seg, segments)


def attend_kernel(n_ctx, n_head, place, sinks, q_ref, bias, w_ref, *rest):
    kv_refs, rest = rest[:n_ctx], rest[n_ctx:]
    outs, (probs, attended, ordered, weights, arrived) = rest[:n_head], rest[n_head:]
    features = weights.shape[0]
    blocks = [(i, min(features, i + COLUMNS)) for i in range(0, features, COLUMNS)]
    copies = [
        pltpu.make_async_copy(
            w_ref.at[pl.ds(i, end - i)], weights.at[pl.ds(i, end - i)], arrived.at[n]
        )
        for n, (i, end) in enumerate(blocks)
    ]
    for copy in copies:
        copy.start()
    tok_count = bias.shape[0]
    own_rows = tok_count // n_head
    kv_width = kv_refs[0].shape[1] // 2
    kv_groups = kv_width // HEAD_SIZE
    share = q_ref.shape[0] // tok_count // kv_groups
    stack = min(share, STACKED_HEADS)
    for g in range(kv_groups):
        ks = slice(g * HEAD_SIZE, (g + 1) * HEAD_SIZE)
        vs = slice(kv_width + g * HEAD_SIZE, kv_width + (g + 1) * HEAD_SIZE)
        k = jnp.concatenate([ref[:, ks] for ref in kv_refs])
        v = jnp.concatenate([ref[:, vs] for ref in kv_refs])
        for j in range(0, share, stack):
            heads = range(g * share + j, g * share + min(share, j + stack))
            scores = dot(q_ref[heads[0] * tok_count : (heads[-1] + 1) * tok_count, :], k, NT)
            denoms = []
            for i, h in enumerate(heads):
                score = scores[i * tok_count : (i + 1) * tok_count] + bias[...]
                top = jnp.maximum(jnp.max(score, axis=1, keepdims=True), sinks[h])
                prob = jnp.exp(score - top)
                denoms.append(jnp.sum(prob, axis=1, keepdims=True) + jnp.exp(sinks[h] - top))
                probs[(j + i) * tok_count : (j + i + 1) * tok_count, :] = prob.astype(jnp.bfloat16)
            out = dot(probs[j * tok_count : (j + len(heads)) * tok_count, :], v, NN)
            for i, h in enumerate(heads):
                attended[:, h * HEAD_SIZE : (h + 1) * HEAD_SIZE] = (
                    out[i * tok_count : (i + 1) * tok_count] / denoms[i]
                ).astype(jnp.bfloat16)
    head = place[1]
    for j in range(n_head):
        source = lax.rem(head + n_head - j, n_head) * own_rows
        ordered[j * own_rows : (j + 1) * own_rows, :] = attended[
            pl.ds(pl.multiple_of(source, own_rows), own_rows), :
        ]
    width = outs[0].shape[1]
    for out in outs:
        out[:, width - LANES :] = jnp.zeros((own_rows, LANES), out.dtype)
    for copy, (i, end) in zip(copies, blocks):
        copy.wait()
        part = dot(ordered[...], weights[i:end, :], NT).astype(jnp.bfloat16)
        for j in range(n_head):
            outs[j][:, i:end] = part[j * own_rows : (j + 1) * own_rows]


def attend(place, sinks, q, bias, w_out_t, kv, n_head, width):
    tok_count, n_keys = bias.shape
    features, columns = w_out_t.shape
    own_rows = tok_count // n_head
    vmem = pl.BlockSpec(memory_space=pltpu.VMEM)
    smem = pl.BlockSpec(memory_space=pltpu.SMEM)
    share = columns // (kv[0].shape[1] // 2)
    return pl.pallas_call(
        functools.partial(attend_kernel, len(kv), n_head),
        out_shape=[jax.ShapeDtypeStruct((own_rows, width), jnp.bfloat16)] * n_head,
        in_specs=[smem, smem, vmem, vmem, pl.BlockSpec(memory_space=pl.ANY)] + [vmem] * len(kv),
        out_specs=[vmem] * n_head,
        scratch_shapes=[
            pltpu.VMEM((share * tok_count, n_keys), jnp.bfloat16),
            pltpu.VMEM((tok_count, columns), jnp.bfloat16),
            pltpu.VMEM((tok_count, columns), jnp.bfloat16),
            pltpu.VMEM(w_out_t.shape, w_out_t.dtype),
            pltpu.SemaphoreType.DMA((-(-features // COLUMNS),)),
        ],
        compiler_params=pltpu.CompilerParams(vmem_limit_bytes=2 * VMEM_LIMIT),
        cost_estimate=pl.CostEstimate(
            flops=4 * tok_count * columns * n_keys + 2 * tok_count * columns * features,
            bytes_accessed=2 * columns * features,
            transcendentals=tok_count * n_keys * columns // HEAD_SIZE,
        ),
        name="attend",
    )(place, sinks, q, bias, in_hbm(w_out_t), *kv)


def norm_kernel(experts, hidden, routes, gain, router, *refs):
    sums, (residual_out, rows_out) = refs[:-2], refs[-2:]
    features = gain.shape[1]
    total = sums[0][...].astype(jnp.float32)
    for other in sums[1:]:
        total = total + other[...].astype(jnp.float32)
    residual = (hidden[...].astype(jnp.float32) + total).astype(jnp.bfloat16)
    residual_out[...] = residual
    widened = residual[:, :features].astype(jnp.float32)
    scale_rows = lax.rsqrt(jnp.mean(widened * widened, axis=-1, keepdims=True) + 1e-05)
    normed = (widened * scale_rows * gain[...]).astype(jnp.bfloat16)
    logits = dot(normed, router[...], NT)
    tail = rows_out.shape[1] - LANES
    offset = features - tail
    lane = lax.broadcasted_iota(jnp.int32, logits.shape, 1)
    expert = lane - offset
    expert = jnp.where(expert >= experts, expert - experts, expert)
    named = routes[:, 0:1] == expert
    for k in range(1, routes.shape[1]):
        named = named | (routes[:, k : k + 1] == expert)
    high_lanes = (lane >= offset) & (lane < offset + experts)
    low_lanes = (lane >= offset + experts) & (lane < offset + 2 * experts)
    chosen = jnp.where(named & (high_lanes | low_lanes), logits, masked_value)
    top = jnp.max(chosen, axis=1, keepdims=True)
    weight = jnp.exp(chosen - top)
    denom = jnp.sum(jnp.where(high_lanes, weight, 0.0), axis=1, keepdims=True)
    gates = weight / denom
    high = gates.astype(jnp.bfloat16).astype(jnp.float32)
    packed = jnp.where(high_lanes, high, jnp.where(low_lanes, gates - high, 0.0))
    rows_out[:, :features] = normed
    end = rows_out[:, tail:].astype(jnp.float32)
    rows_out[:, tail:] = jnp.where(lane < offset, end, packed).astype(jnp.bfloat16)


def norm_and_gates(sums, hidden, routes, gain, router_lanes, experts):
    rows, width = hidden.shape
    features = gain.shape[1]
    vmem = pl.BlockSpec(memory_space=pltpu.VMEM)
    return pl.pallas_call(
        functools.partial(norm_kernel, experts),
        out_shape=[jax.ShapeDtypeStruct((rows, width), jnp.bfloat16)] * 2,
        in_specs=[vmem] * (4 + len(sums)),
        out_specs=[vmem] * 2,
        compiler_params=pltpu.CompilerParams(vmem_limit_bytes=VMEM_LIMIT),
        cost_estimate=pl.CostEstimate(
            flops=rows * features * LANES * 2,
            bytes_accessed=rows * features * 10,
            transcendentals=rows * LANES,
        ),
        name="norm_and_gates",
    )(hidden, routes, gain, router_lanes, *sums)


def expert_kernel(experts, n_head, place, gate_up, down, flag, *refs):
    near, far = refs[:n_head], refs[n_head : 2 * n_head]
    outs, (far_out, done, rows, hidden) = refs[2 * n_head : -4], refs[-4:]
    done[...] = flag[...]
    units, features = down.shape
    count, width = near[0].shape
    tail = width - LANES
    lane = lax.broadcasted_iota(jnp.int32, (count, LANES), 1) - (features - tail)
    mine = (lane == place[0]) | (lane == place[0] + experts)
    gates = []
    for i, ref in enumerate(near + far):
        rows[i * count : (i + 1) * count, :] = ref[:, :features]
        packed = ref[:, tail:].astype(jnp.float32)
        gates.append(jnp.sum(jnp.where(mine, packed, 0.0), axis=1, keepdims=True))
    for ref in (*outs, far_out):
        ref[:, tail:] = jnp.zeros((ref.shape[0], LANES), ref.dtype)
    parts, _, block = hidden.shape

    def some_units(n, carry):
        here = pl.ds(pl.multiple_of(n * block, BF16_ROWS), block) if parts > 1 else slice(None)
        gate_pre = dot(rows[...], gate_up[0, here, :], NT)
        up_pre = dot(rows[...], gate_up[1, here, :], NT)
        act = gate_pre * jax.nn.sigmoid(1.702 * gate_pre) * (up_pre + 1.0)
        hidden[n] = act.astype(jnp.bfloat16)
        return carry

    lax.fori_loop(0, parts, some_units, 0)
    units_by_row = jnp.concatenate([hidden[n] for n in range(parts)], axis=1)
    for i in range(0, features, COLUMNS):
        end = min(features, i + COLUMNS)
        part = dot(units_by_row, down[:, i:end], NN)
        for j in range(2 * n_head):
            block = (part[j * count : (j + 1) * count] * gates[j]).astype(jnp.bfloat16)
            if j < n_head:
                outs[j][:, i:end] = block
            else:
                far_out[(j - n_head) * count : (j - n_head + 1) * count, i:end] = block


def expert_rows(
                place, near, far, gate_up_t, down, flag, experts
            ):
    count, width = near[0].shape
    units, features = down.shape
    n_head = len(near)
    parts = UNIT_PARTS if units % (UNIT_PARTS * BF16_ROWS) == 0 else 1
    vmem = pl.BlockSpec(memory_space=pltpu.VMEM)
    return pl.pallas_call(
        functools.partial(expert_kernel, experts, n_head),
        out_shape=[jax.ShapeDtypeStruct((count, width), jnp.bfloat16)] * n_head
        + [jax.ShapeDtypeStruct((n_head * count, width), jnp.bfloat16)]
        + [jax.ShapeDtypeStruct(flag.shape, flag.dtype)],
        in_specs=[pl.BlockSpec(memory_space=pltpu.SMEM)] + [vmem] * (3 + 2 * n_head),
        out_specs=[vmem] * (n_head + 2),
        scratch_shapes=[
            pltpu.VMEM((2 * n_head * count, features), jnp.bfloat16),
            pltpu.VMEM((parts, 2 * n_head * count, units // parts), jnp.bfloat16),
        ],
        compiler_params=pltpu.CompilerParams(vmem_limit_bytes=VMEM_LIMIT),
        cost_estimate=pl.CostEstimate(
            flops=12 * n_head * count * units * features,
            bytes_accessed=6 * units * features,
            transcendentals=2 * n_head * count * units,
        ),
        name="expert_rows",
    )(place, in_vmem(gate_up_t), in_vmem(down), flag, *near, *far)


def finish_kernel(n_halves, flag, *refs):
    terms, halves, out = refs[: len(refs) - 1 - n_halves], refs[len(refs) - 1 - n_halves : -1], refs[-1]
    features = out.shape[1]
    start = 0
    for half in halves or terms[:1]:
        end = min(features, start + half.shape[1])
        total = half[:, : end - start].astype(jnp.float32)
        for term in terms if halves else terms[1:]:
            total = total + term[:, start:end].astype(jnp.float32)
        out[:, start:end] = total.astype(out.dtype)
        start = end


def finish(flag, terms, halves, features):
    vmem = pl.BlockSpec(memory_space=pltpu.VMEM)
    rows, width = terms[0].shape
    return pl.pallas_call(
        functools.partial(finish_kernel, len(halves)),
        out_shape=jax.ShapeDtypeStruct((rows, features), terms[0].dtype),
        in_specs=[vmem] * (1 + len(terms) + len(halves)),
        out_specs=vmem,
        compiler_params=pltpu.CompilerParams(vmem_limit_bytes=VMEM_LIMIT),
        cost_estimate=pl.CostEstimate(
            flops=rows * width * (len(terms) + 1),
            bytes_accessed=rows * width * 2 * (len(terms) + 2),
            transcendentals=0,
        ),
        name="finish",
    )(flag, *terms, *halves)


def body(
    queries,
    keys,
    values,
    sinks,
    segments,
    hidden_in,
    routes,
    w_out,
    norm_gain,
    router,
    w_gate_up,
    w_down,
):
    n_ctx = lax.axis_size("ctx")
    n_head = lax.axis_size("head")
    n_z = n_ctx // CORES
    ctx = lax.axis_index("ctx")
    head = lax.axis_index("head")
    tok_count = queries.shape[0]
    features = hidden_in.shape[1]
    experts = router.shape[1]
    own_rows = tok_count // n_head
    width = -(-(features + 2 * experts) // LANES) * LANES

    to_sibling = [(i, i ^ 1) for i in range(n_ctx)]
    ring = list(range(0, n_z, 2))
    ring = ring[::-1] + list(range(1, n_z, 2))
    follower = {ring[i]: ring[(i + 1) % n_z] for i in range(n_z)}
    to_next_chip = [(i, follower[i // CORES] * CORES + i % CORES) for i in range(n_ctx)]

    def sibling(x):
        return lax.ppermute(x, "ctx", to_sibling)

    def next_chip(x):
        return lax.ppermute(x, "ctx", to_next_chip)

    def next_head(x, j):
        return lax.ppermute(x, "head", [(i, (i + j) % n_head) for i in range(n_head)])

    def add(*terms):
        total = terms[0].astype(jnp.float32)
        for term in terms[1:]:
            total = total + term.astype(jnp.float32)
        return total.astype(jnp.bfloat16)

    def after(later, earlier):
        return lax.optimization_barrier((later, earlier))

    place = jnp.stack([ctx, head]).astype(jnp.int32)
    row_start = head * own_rows
    own_hidden = jnp.pad(
        lax.dynamic_slice_in_dim(hidden_in, row_start, own_rows, 0), ((0, 0), (0, width - features))
    )
    own_routes = lax.dynamic_slice_in_dim(routes, row_start, own_rows, 0)
    tok_seg = lax.dynamic_slice_in_dim(segments, ctx * tok_count, tok_count, 0)[:, None]
    tail = features - (width - LANES)
    router_lanes = jnp.pad(
        jnp.concatenate([router.T, router.T]), ((tail, LANES - tail - 2 * experts), (0, 0))
    )

    with jax.named_scope("keys_and_values"):
        own = side_by_side(keys, values)
        kv = [
            lax.ppermute(own, "ctx", [(i, i + CORES * k) for i in range(n_ctx - CORES * k)])
            for k in range(n_z - 1, 0, -1)
        ]
        kv = [own] + kv[::-1]
    with jax.named_scope("attention"):
        q, bias = prepare(place, queries, tok_seg, segments[None, :])
        kv, q = after(kv, q)
        kv = [x for one in kv for x in (one, sibling(one))]
        sums = attend(place, sinks, q, bias, w_out.T, kv, n_head, width)

    with jax.named_scope("norm"):
        gathered = [sums[0]] + [next_head(sums[j], n_head - j) for j in range(1, n_head)]
        down, gate_up_t, flag = load([w_down[0], jnp.swapaxes(w_gate_up[0], 1, 2)], sums[0])
        gathered, flag = after(gathered, flag)
        residual, rows = norm_and_gates(
            gathered, own_hidden, own_routes, norm_gain[None, :], router_lanes, experts
        )

    def to_heads(x):
        return [x] + [next_head(x, j) for j in range(1, n_head)]

    def to_other_heads(sums):
        return [next_head(sums[j - 1], n_head - j) for j in range(1, n_head)]

    with jax.named_scope("rows_of_chips"):
        near = to_heads(rows)
        chunk = next_chip(rows)
        near, chunk, flag = lax.optimization_barrier((near, chunk, flag))

    middle = -(-width // LANES // 2) * LANES
    halves = [slice(0, middle), slice(middle, width)]
    waiting, arriving = None, []
    for hop in range(n_z):
        with jax.named_scope("rows_of_chips"):
            lot, coming = None, None
            if hop < n_z - 2 or hop == 0 and n_z > 1:
                lot = to_heads(chunk)
                coming = next_chip(chunk) if hop < n_z - 2 else None
            elif hop == n_z - 2:
                lot = [chunk] + [next_chip(x) for x in near[1:]]
        with jax.named_scope("experts"):
            far = [sibling(x) for x in near]
            *near_out, far_out, flag = expert_rows(
                place, near, far, gate_up_t, down, flag, experts
            )
        with jax.named_scope("sum_back"):
            lot, coming, waiting, arriving, far_out = lax.optimization_barrier(
                (lot, coming, waiting, arriving, far_out)
            )
            if waiting is not None:
                sent = halves if hop == n_z - 1 else [slice(0, width)]
                arriving = [
                    next_chip(add(*[x[:, part] for x in (*waiting, *arriving)])) for part in sent
                ]
            crossed = sibling(far_out)
            blocks = [
                (near_out[j], crossed[j * own_rows : (j + 1) * own_rows]) for j in range(n_head)
            ]
            if hop == 0:
                own_blocks = blocks
            elif hop < n_z - 1:
                leaving = [add(*block) for block in blocks[1:]]
                leaving, flag = after(leaving, flag)
                waiting = [*blocks[0], *to_other_heads(leaving)]
            near, chunk = lot, coming

    with jax.named_scope("sum_back"):
        if n_z > 1:
            others = [[add(*[x[:, half] for x in b]) for b in blocks[1:]] for half in halves]
            crossing = [to_other_heads(x) for x in others]
            crossing[0], own_blocks = after(crossing[0], own_blocks)
            arriving = [
                next_chip(
                    add(*[x[:, half] for x in blocks[0]], *crossing[i], *arriving[i : i + 1])
                )
                for i, half in enumerate(halves)
            ]
        own_sums = to_other_heads([add(*block) for block in own_blocks[1:]])
        return finish(flag, [*own_blocks[0], residual, *own_sums], arriving, features)


def solution(mesh):
    placed = (
        P(("group", "ctx"), "head"),
        P(("group", "ctx"), "head"),
        P(("group", "ctx"), "head"),
        P("head"),
        P("group"),
        P(("group", "ctx"), None),
        P(("group", "ctx"), None),
        P("head", None),
        P(),
        P(),
        P("ctx", None, None, "head"),
        P("ctx", "head", None),
    )
    return jax.shard_map(
        body,
        mesh=mesh,
        in_specs=placed,
        out_specs=P(("group", "ctx", "head"), None),
        check_vma=False,
    )
```

```python
import functools

import jax
import jax.numpy as jnp
from jax import lax
from jax.experimental import pallas as pl
from jax.experimental.pallas import tpu as pltpu
from jax.sharding import PartitionSpec as P

HEAD_SIZE = 64
LANES = 128
CORES = 2
VMEM_LIMIT = 16 << 20
STACKED_HEADS = 4
UNIT_PARTS = 2
BF16_ROWS = 16
COLUMNS = 12 * LANES

masked_value = -1e30
NT = (((1,), (1,)), ((), ()))
NN = (((1,), (0,)), ((), ()))


def dot(a, b, dims):
    return lax.dot_general(a, b, dims, preferred_element_type=jnp.float32)


def load_kernel(n, *refs):
    sources, targets, flag, arrived = refs[:n], refs[-n - 2 : -2], refs[-2], refs[-1]
    flag[...] = jnp.zeros(flag.shape, flag.dtype)
    copies = [pltpu.make_async_copy(sources[i], targets[i], arrived.at[i]) for i in range(n)]
    for copy in copies:
        copy.start()
    for copy in copies:
        copy.wait()


def load(arrays, earlier):
    n = len(arrays)
    return pl.pallas_call(
        functools.partial(load_kernel, n),
        out_shape=[pltpu.VMEM(a.shape, a.dtype) for a in arrays]
        + [jax.ShapeDtypeStruct((8, LANES), jnp.float32)],
        in_specs=[pl.BlockSpec(memory_space=pl.ANY)] * n
        + [pl.BlockSpec(memory_space=pltpu.VMEM)],
        out_specs=[pl.BlockSpec(memory_space=pltpu.VMEM)] * (n + 1),
        scratch_shapes=[pltpu.SemaphoreType.DMA((n,))],
        compiler_params=pltpu.CompilerParams(vmem_limit_bytes=VMEM_LIMIT),
        cost_estimate=pl.CostEstimate(
            flops=0, bytes_accessed=sum(4 * a.size for a in arrays), transcendentals=0
        ),
        name="load",
    )(*[in_hbm(a) for a in arrays], earlier)


def in_hbm(x):
    return pltpu.with_memory_space_constraint(x, pltpu.HBM)


def in_vmem(x):
    return pltpu.with_memory_space_constraint(x, pltpu.VMEM)


def pack_kernel(left, right, both, arrived):
    half = left.shape[1]
    if half % LANES:
        both[:, :half] = left[...]
        both[:, half:] = right[...]
        return
    copies = [
        pltpu.make_async_copy(left, both.at[:, pl.ds(0, half)], arrived.at[0]),
        pltpu.make_async_copy(right, both.at[:, pl.ds(half, half)], arrived.at[1]),
    ]
    for copy in copies:
        copy.start()
    for copy in copies:
        copy.wait()


def side_by_side(left, right):
    rows, half = left.shape
    vmem = pl.BlockSpec(memory_space=pltpu.VMEM)
    source = vmem if half % LANES else pl.BlockSpec(memory_space=pl.ANY)
    return pl.pallas_call(
        pack_kernel,
        out_shape=jax.ShapeDtypeStruct((rows, 2 * half), left.dtype),
        in_specs=[source] * 2,
        out_specs=vmem,
        scratch_shapes=[pltpu.SemaphoreType.DMA((2,))],
        compiler_params=pltpu.CompilerParams(vmem_limit_bytes=VMEM_LIMIT),
        cost_estimate=pl.CostEstimate(
            flops=0, bytes_accessed=8 * rows * half, transcendentals=0
        ),
        name="side_by_side",
    )(*[x if half % LANES else in_hbm(x) for x in (left, right)])


def prepare_kernel(place, q_ref, tok_seg, segments, q_out, bias):
    tok_count = q_ref.shape[0]
    for h in range(q_ref.shape[1] // HEAD_SIZE):
        q_out[h * tok_count : (h + 1) * tok_count, :] = q_ref[
            :, h * HEAD_SIZE : (h + 1) * HEAD_SIZE
        ] * jnp.asarray(HEAD_SIZE**-0.5, q_ref.dtype)
    ctx = place[0]
    z_here = ctx // CORES
    core = ctx - z_here * CORES
    first = jnp.sum((segments[...] < tok_seg[...]).astype(jnp.float32), axis=1, keepdims=True)
    tok = ctx * tok_count + lax.broadcasted_iota(jnp.int32, bias.shape, 0)
    lane = lax.broadcasted_iota(jnp.int32, bias.shape, 1)
    block = lane // tok_count
    hop = block // CORES
    owner = (z_here - hop) * CORES + jnp.where(block == hop * CORES, core, 1 - core)
    pos = owner * tok_count + (lane - block * tok_count)
    seen = (z_here >= hop) & (pos <= tok) & (pos.astype(jnp.float32) >= first)
    bias[...] = jnp.where(seen, 0.0, masked_value)


def prepare(place, q, tok_seg, segments):
    tok_count, columns = q.shape
    vmem = pl.BlockSpec(memory_space=pltpu.VMEM)
    return pl.pallas_call(
        prepare_kernel,
        out_shape=[
            jax.ShapeDtypeStruct((columns // HEAD_SIZE * tok_count, HEAD_SIZE), q.dtype),
            jax.ShapeDtypeStruct((tok_count, segments.shape[1]), jnp.float32),
        ],
        in_specs=[pl.BlockSpec(memory_space=pltpu.SMEM)] + [vmem] * 3,
        out_specs=[vmem] * 2,
        compiler_params=pltpu.CompilerParams(vmem_limit_bytes=VMEM_LIMIT),
        cost_estimate=pl.CostEstimate(
            flops=20 * tok_count * segments.shape[1],
            bytes_accessed=4 * tok_count * segments.shape[1],
            transcendentals=0,
        ),
        name="prepare",
    )(place, q, tok_seg, segments)


def attend_kernel(n_ctx, n_head, place, sinks, q_ref, bias, w_ref, *rest):
    kv_refs, rest = rest[:n_ctx], rest[n_ctx:]
    outs, (probs, attended, ordered, weights, arrived) = rest[:n_head], rest[n_head:]
    features = weights.shape[0]
    blocks = [(i, min(features, i + COLUMNS)) for i in range(0, features, COLUMNS)]
    copies = [
        pltpu.make_async_copy(
            w_ref.at[pl.ds(i, end - i)], weights.at[pl.ds(i, end - i)], arrived.at[n]
        )
        for n, (i, end) in enumerate(blocks)
    ]
    for copy in copies:
        copy.start()
    tok_count = bias.shape[0]
    own_rows = tok_count // n_head
    kv_width = kv_refs[0].shape[1] // 2
    kv_groups = kv_width // HEAD_SIZE
    share = q_ref.shape[0] // tok_count // kv_groups
    stack = min(share, STACKED_HEADS)
    for g in range(kv_groups):
        ks = slice(g * HEAD_SIZE, (g + 1) * HEAD_SIZE)
        vs = slice(kv_width + g * HEAD_SIZE, kv_width + (g + 1) * HEAD_SIZE)
        k = jnp.concatenate([ref[:, ks] for ref in kv_refs])
        v = jnp.concatenate([ref[:, vs] for ref in kv_refs])
        for j in range(0, share, stack):
            heads = range(g * share + j, g * share + min(share, j + stack))
            scores = dot(q_ref[heads[0] * tok_count : (heads[-1] + 1) * tok_count, :], k, NT)
            denoms = []
            for i, h in enumerate(heads):
                score = scores[i * tok_count : (i + 1) * tok_count] + bias[...]
                top = jnp.maximum(jnp.max(score, axis=1, keepdims=True), sinks[h])
                prob = jnp.exp(score - top)
                denoms.append(jnp.sum(prob, axis=1, keepdims=True) + jnp.exp(sinks[h] - top))
                probs[(j + i) * tok_count : (j + i + 1) * tok_count, :] = prob.astype(jnp.bfloat16)
            out = dot(probs[j * tok_count : (j + len(heads)) * tok_count, :], v, NN)
            for i, h in enumerate(heads):
                attended[:, h * HEAD_SIZE : (h + 1) * HEAD_SIZE] = (
                    out[i * tok_count : (i + 1) * tok_count] / denoms[i]
                ).astype(jnp.bfloat16)
    head = place[1]
    for j in range(n_head):
        source = lax.rem(head + n_head - j, n_head) * own_rows
        ordered[j * own_rows : (j + 1) * own_rows, :] = attended[
            pl.ds(pl.multiple_of(source, own_rows), own_rows), :
        ]
    width = outs[0].shape[1]
    for out in outs:
        out[:, width - LANES :] = jnp.zeros((own_rows, LANES), out.dtype)
    for copy, (i, end) in zip(copies, blocks):
        copy.wait()
        part = dot(ordered[...], weights[i:end, :], NT).astype(jnp.bfloat16)
        for j in range(n_head):
            outs[j][:, i:end] = part[j * own_rows : (j + 1) * own_rows]


def attend(place, sinks, q, bias, w_out_t, kv, n_head, width):
    tok_count, n_keys = bias.shape
    features, columns = w_out_t.shape
    own_rows = tok_count // n_head
    vmem = pl.BlockSpec(memory_space=pltpu.VMEM)
    smem = pl.BlockSpec(memory_space=pltpu.SMEM)
    share = columns // (kv[0].shape[1] // 2)
    return pl.pallas_call(
        functools.partial(attend_kernel, len(kv), n_head),
        out_shape=[jax.ShapeDtypeStruct((own_rows, width), jnp.bfloat16)] * n_head,
        in_specs=[smem, smem, vmem, vmem, pl.BlockSpec(memory_space=pl.ANY)] + [vmem] * len(kv),
        out_specs=[vmem] * n_head,
        scratch_shapes=[
            pltpu.VMEM((share * tok_count, n_keys), jnp.bfloat16),
            pltpu.VMEM((tok_count, columns), jnp.bfloat16),
            pltpu.VMEM((tok_count, columns), jnp.bfloat16),
            pltpu.VMEM(w_out_t.shape, w_out_t.dtype),
            pltpu.SemaphoreType.DMA((-(-features // COLUMNS),)),
        ],
        compiler_params=pltpu.CompilerParams(vmem_limit_bytes=2 * VMEM_LIMIT),
        cost_estimate=pl.CostEstimate(
            flops=4 * tok_count * columns * n_keys + 2 * tok_count * columns * features,
            bytes_accessed=2 * columns * features,
            transcendentals=tok_count * n_keys * columns // HEAD_SIZE,
        ),
        name="attend",
    )(place, sinks, q, bias, in_hbm(w_out_t), *kv)


def norm_kernel(experts, hidden, routes, gain, router, *refs):
    sums, (residual_out, rows_out) = refs[:-2], refs[-2:]
    features = gain.shape[1]
    total = sums[0][...].astype(jnp.float32)
    for other in sums[1:]:
        total = total + other[...].astype(jnp.float32)
    residual = (hidden[...].astype(jnp.float32) + total).astype(jnp.bfloat16)
    residual_out[...] = residual
    widened = residual[:, :features].astype(jnp.float32)
    scale_rows = lax.rsqrt(jnp.mean(widened * widened, axis=-1, keepdims=True) + 1e-05)
    normed = (widened * scale_rows * gain[...]).astype(jnp.bfloat16)
    logits = dot(normed, router[...], NT)
    tail = rows_out.shape[1] - LANES
    offset = features - tail
    lane = lax.broadcasted_iota(jnp.int32, logits.shape, 1)
    expert = lane - offset
    expert = jnp.where(expert >= experts, expert - experts, expert)
    named = routes[:, 0:1] == expert
    for k in range(1, routes.shape[1]):
        named = named | (routes[:, k : k + 1] == expert)
    high_lanes = (lane >= offset) & (lane < offset + experts)
    low_lanes = (lane >= offset + experts) & (lane < offset + 2 * experts)
    chosen = jnp.where(named & (high_lanes | low_lanes), logits, masked_value)
    top = jnp.max(chosen, axis=1, keepdims=True)
    weight = jnp.exp(chosen - top)
    denom = jnp.sum(jnp.where(high_lanes, weight, 0.0), axis=1, keepdims=True)
    gates = weight / denom
    high = gates.astype(jnp.bfloat16).astype(jnp.float32)
    packed = jnp.where(high_lanes, high, jnp.where(low_lanes, gates - high, 0.0))
    rows_out[:, :features] = normed
    end = rows_out[:, tail:].astype(jnp.float32)
    rows_out[:, tail:] = jnp.where(lane < offset, end, packed).astype(jnp.bfloat16)


def norm_and_gates(sums, hidden, routes, gain, router_lanes, experts):
    rows, width = hidden.shape
    features = gain.shape[1]
    vmem = pl.BlockSpec(memory_space=pltpu.VMEM)
    return pl.pallas_call(
        functools.partial(norm_kernel, experts),
        out_shape=[jax.ShapeDtypeStruct((rows, width), jnp.bfloat16)] * 2,
        in_specs=[vmem] * (4 + len(sums)),
        out_specs=[vmem] * 2,
        compiler_params=pltpu.CompilerParams(vmem_limit_bytes=VMEM_LIMIT),
        cost_estimate=pl.CostEstimate(
            flops=rows * features * LANES * 2,
            bytes_accessed=rows * features * 10,
            transcendentals=rows * LANES,
        ),
        name="norm_and_gates",
    )(hidden, routes, gain, router_lanes, *sums)


def expert_kernel(experts, n_head, place, gate_up, down, flag, *refs):
    near, far = refs[:n_head], refs[n_head : 2 * n_head]
    outs, (far_out, done, rows, hidden) = refs[2 * n_head : -4], refs[-4:]
    done[...] = flag[...]
    units, features = down.shape
    count, width = near[0].shape
    tail = width - LANES
    lane = lax.broadcasted_iota(jnp.int32, (count, LANES), 1) - (features - tail)
    mine = (lane == place[0]) | (lane == place[0] + experts)
    gates = []
    for i, ref in enumerate(near + far):
        rows[i * count : (i + 1) * count, :] = ref[:, :features]
        packed = ref[:, tail:].astype(jnp.float32)
        gates.append(jnp.sum(jnp.where(mine, packed, 0.0), axis=1, keepdims=True))
    for ref in (*outs, far_out):
        ref[:, tail:] = jnp.zeros((ref.shape[0], LANES), ref.dtype)
    parts, _, block = hidden.shape

    def some_units(n, carry):
        here = pl.ds(pl.multiple_of(n * block, BF16_ROWS), block) if parts > 1 else slice(None)
        gate_pre = dot(rows[...], gate_up[0, here, :], NT)
        up_pre = dot(rows[...], gate_up[1, here, :], NT)
        act = gate_pre * jax.nn.sigmoid(1.702 * gate_pre) * (up_pre + 1.0)
        hidden[n] = act.astype(jnp.bfloat16)
        return carry

    lax.fori_loop(0, parts, some_units, 0)
    units_by_row = jnp.concatenate([hidden[n] for n in range(parts)], axis=1)
    for i in range(0, features, COLUMNS):
        end = min(features, i + COLUMNS)
        part = dot(units_by_row, down[:, i:end], NN)
        for j in range(2 * n_head):
            block = (part[j * count : (j + 1) * count] * gates[j]).astype(jnp.bfloat16)
            if j < n_head:
                outs[j][:, i:end] = block
            else:
                far_out[(j - n_head) * count : (j - n_head + 1) * count, i:end] = block


def expert_rows(
                place, near, far, gate_up_t, down, flag, experts
            ):
    count, width = near[0].shape
    units, features = down.shape
    n_head = len(near)
    parts = UNIT_PARTS if units % (UNIT_PARTS * BF16_ROWS) == 0 else 1
    vmem = pl.BlockSpec(memory_space=pltpu.VMEM)
    return pl.pallas_call(
        functools.partial(expert_kernel, experts, n_head),
        out_shape=[jax.ShapeDtypeStruct((count, width), jnp.bfloat16)] * n_head
        + [jax.ShapeDtypeStruct((n_head * count, width), jnp.bfloat16)]
        + [jax.ShapeDtypeStruct(flag.shape, flag.dtype)],
        in_specs=[pl.BlockSpec(memory_space=pltpu.SMEM)] + [vmem] * (3 + 2 * n_head),
        out_specs=[vmem] * (n_head + 2),
        scratch_shapes=[
            pltpu.VMEM((2 * n_head * count, features), jnp.bfloat16),
            pltpu.VMEM((parts, 2 * n_head * count, units // parts), jnp.bfloat16),
        ],
        compiler_params=pltpu.CompilerParams(vmem_limit_bytes=VMEM_LIMIT),
        cost_estimate=pl.CostEstimate(
            flops=12 * n_head * count * units * features,
            bytes_accessed=6 * units * features,
            transcendentals=2 * n_head * count * units,
        ),
        name="expert_rows",
    )(place, in_vmem(gate_up_t), in_vmem(down), flag, *near, *far)


def finish_kernel(n_halves, flag, *refs):
    terms, halves, out = refs[: len(refs) - 1 - n_halves], refs[len(refs) - 1 - n_halves : -1], refs[-1]
    features = out.shape[1]
    start = 0
    for half in halves or terms[:1]:
        end = min(features, start + half.shape[1])
        total = half[:, : end - start].astype(jnp.float32)
        for term in terms if halves else terms[1:]:
            total = total + term[:, start:end].astype(jnp.float32)
        out[:, start:end] = total.astype(out.dtype)
        start = end


def finish(flag, terms, halves, features):
    vmem = pl.BlockSpec(memory_space=pltpu.VMEM)
    rows, width = terms[0].shape
    return pl.pallas_call(
        functools.partial(finish_kernel, len(halves)),
        out_shape=jax.ShapeDtypeStruct((rows, features), terms[0].dtype),
        in_specs=[vmem] * (1 + len(terms) + len(halves)),
        out_specs=vmem,
        compiler_params=pltpu.CompilerParams(vmem_limit_bytes=VMEM_LIMIT),
        cost_estimate=pl.CostEstimate(
            flops=rows * width * (len(terms) + 1),
            bytes_accessed=rows * width * 2 * (len(terms) + 2),
            transcendentals=0,
        ),
        name="finish",
    )(flag, *terms, *halves)


def body(
    queries,
    keys,
    values,
    sinks,
    segments,
    hidden_in,
    routes,
    w_out,
    norm_gain,
    router,
    w_gate_up,
    w_down,
):
    n_ctx = lax.axis_size("ctx")
    n_head = lax.axis_size("head")
    n_z = n_ctx // CORES
    ctx = lax.axis_index("ctx")
    head = lax.axis_index("head")
    tok_count = queries.shape[0]
    features = hidden_in.shape[1]
    experts = router.shape[1]
    own_rows = tok_count // n_head
    width = -(-(features + 2 * experts) // LANES) * LANES

    to_sibling = [(i, i ^ 1) for i in range(n_ctx)]
    ring = list(range(0, n_z, 2))
    ring = ring[::-1] + list(range(1, n_z, 2))
    follower = {ring[i]: ring[(i + 1) % n_z] for i in range(n_z)}
    to_next_chip = [(i, follower[i // CORES] * CORES + i % CORES) for i in range(n_ctx)]

    def sibling(x):
        return lax.ppermute(x, "ctx", to_sibling)

    def next_chip(x):
        return lax.ppermute(x, "ctx", to_next_chip)

    def next_head(x, j):
        return lax.ppermute(x, "head", [(i, (i + j) % n_head) for i in range(n_head)])

    def add(*terms):
        total = terms[0].astype(jnp.float32)
        for term in terms[1:]:
            total = total + term.astype(jnp.float32)
        return total.astype(jnp.bfloat16)

    def after(later, earlier):
        return lax.optimization_barrier((later, earlier))

    place = jnp.stack([ctx, head]).astype(jnp.int32)
    row_start = head * own_rows
    own_hidden = jnp.pad(
        lax.dynamic_slice_in_dim(hidden_in, row_start, own_rows, 0), ((0, 0), (0, width - features))
    )
    own_routes = lax.dynamic_slice_in_dim(routes, row_start, own_rows, 0)
    tok_seg = lax.dynamic_slice_in_dim(segments, ctx * tok_count, tok_count, 0)[:, None]
    tail = features - (width - LANES)
    router_lanes = jnp.pad(
        jnp.concatenate([router.T, router.T]), ((tail, LANES - tail - 2 * experts), (0, 0))
    )

    with jax.named_scope("keys_and_values"):
        own = side_by_side(keys, values)
        kv = [
            lax.ppermute(own, "ctx", [(i, i + CORES * k) for i in range(n_ctx - CORES * k)])
            for k in range(n_z - 1, 0, -1)
        ]
        kv = [own] + kv[::-1]
    with jax.named_scope("attention"):
        q, bias = prepare(place, queries, tok_seg, segments[None, :])
        kv, q = after(kv, q)
        kv = [x for one in kv for x in (one, sibling(one))]
        sums = attend(place, sinks, q, bias, w_out.T, kv, n_head, width)

    with jax.named_scope("norm"):
        gathered = [sums[0]] + [next_head(sums[j], n_head - j) for j in range(1, n_head)]
        down, gate_up_t, flag = load([w_down[0], jnp.swapaxes(w_gate_up[0], 1, 2)], sums[0])
        gathered, flag = after(gathered, flag)
        residual, rows = norm_and_gates(
            gathered, own_hidden, own_routes, norm_gain[None, :], router_lanes, experts
        )

    def to_heads(x):
        return [x] + [next_head(x, j) for j in range(1, n_head)]

    def to_other_heads(sums):
        return [next_head(sums[j - 1], n_head - j) for j in range(1, n_head)]

    with jax.named_scope("rows_of_chips"):
        near = to_heads(rows)
        chunk = next_chip(rows)
        near, chunk, flag = lax.optimization_barrier((near, chunk, flag))

    middle = -(-width // LANES // 3) * LANES
    halves = [slice(0, middle), slice(middle, width)]
    waiting, arriving = None, []
    for hop in range(n_z):
        with jax.named_scope("rows_of_chips"):
            lot, coming = None, None
            if hop < n_z - 2 or hop == 0 and n_z > 1:
                lot = to_heads(chunk)
                coming = next_chip(chunk) if hop < n_z - 2 else None
            elif hop == n_z - 2:
                lot = [chunk] + [next_chip(x) for x in near[1:]]
        with jax.named_scope("experts"):
            far = [sibling(x) for x in near]
            *near_out, far_out, flag = expert_rows(
                place, near, far, gate_up_t, down, flag, experts
            )
        with jax.named_scope("sum_back"):
            lot, coming, waiting, arriving, far_out = lax.optimization_barrier(
                (lot, coming, waiting, arriving, far_out)
            )
            if waiting is not None:
                sent = halves if hop == n_z - 1 else [slice(0, width)]
                arriving = [
                    next_chip(add(*[x[:, part] for x in (*waiting, *arriving)])) for part in sent
                ]
            crossed = sibling(far_out)
            blocks = [
                (near_out[j], crossed[j * own_rows : (j + 1) * own_rows]) for j in range(n_head)
            ]
            if hop == 0:
                own_blocks = blocks
            elif hop < n_z - 1:
                leaving = [add(*block) for block in blocks[1:]]
                leaving, flag = after(leaving, flag)
                waiting = [*blocks[0], *to_other_heads(leaving)]
            near, chunk = lot, coming

    with jax.named_scope("sum_back"):
        if n_z > 1:
            others = [[add(*[x[:, half] for x in b]) for b in blocks[1:]] for half in halves]
            crossing = [to_other_heads(x) for x in others]
            crossing[0], own_blocks = after(crossing[0], own_blocks)
            arriving = [
                next_chip(
                    add(*[x[:, half] for x in blocks[0]], *crossing[i], *arriving[i : i + 1])
                )
                for i, half in enumerate(halves)
            ]
        own_sums = to_other_heads([add(*block) for block in own_blocks[1:]])
        return finish(flag, [*own_blocks[0], residual, *own_sums], arriving, features)


def solution(mesh):
    placed = (
        P(("group", "ctx"), "head"),
        P(("group", "ctx"), "head"),
        P(("group", "ctx"), "head"),
        P("head"),
        P("group"),
        P(("group", "ctx"), None),
        P(("group", "ctx"), None),
        P("head", None),
        P(),
        P(),
        P("ctx", None, None, "head"),
        P("ctx", "head", None),
    )
    return jax.shard_map(
        body,
        mesh=mesh,
        in_specs=placed,
        out_specs=P(("group", "ctx", "head"), None),
        check_vma=False,
    )
```
